32 devices in a mesh: lon: 16 (over z, x, core), lat: 2 (over y).
Axes of the slice: x: 2, y: 2, z: 4, core: 2. Of those that a mesh axis runs over, the one named last changes fastest.
Arguments:
- potential_heat: float32 [8, 256, 2048], P(None, 'lat', 'lon'), may hold values from -6 to 6
- saltiness_anomaly: float32 [8, 256, 2048], P(None, 'lat', 'lon'), may hold values from -6 to 6
- east_current: float32 [8, 256, 2048], P(None, 'lat', 'lon'), may hold values from -1 to 1
- north_current: float32 [8, 256, 2048], P(None, 'lat', 'lon'), may hold values from -1 to 1
- water_indicator: int32 [8, 256, 2048], P(None, 'lat', 'lon'), may hold values from 0 to 1, as said below
- east_west_courant_factor: float32 [256, 2048], P('lat', 'lon'), may hold values from 0.05 to 0.45
- north_south_courant_factor: float32 [256, 2048], P('lat', 'lon'), may hold values from 0.05 to 0.45
- interface_diffusion_factor: float32 [7, 256, 2048], P(None, 'lat', 'lon'), may hold values from 0.05 to 5
- spreading_coefficient: float32 [4, 8], replicated, may hold values from 0.05 to 0.25
- seam_mirror_index: int32 [2048], P('lon'), may hold values from 0 to 2047, as said below
Outputs:
- temperature_next: float32 [8, 256, 2048], P(None, 'lat', 'lon')
- salinity_next: float32 [8, 256, 2048], P(None, 'lat', 'lon')
- zonal_next: float32 [8, 256, 2048], P(None, 'lat', 'lon')
- meridional_next: float32 [8, 256, 2048], P(None, 'lat', 'lon')
The draws below stay inside these ranges and needn't reach their ends.
Inputs may be any that keep to these rules, and one draw needn't show every extreme that they name: water_indicator is 0 or 1, and a cell below a land cell is land. seam_mirror_index[i] = (p - i) mod 2048 for one p whose remainder on division by 128 is 127.
All inputs are finite; a program needn't handle non-finite values.
Results may differ from the reference program's by a relative error of at most 0.0003.
Values sent between devices are 32-bit elements; how exact they have to be, the bound alone decides.
A program may use at most 128 MiB of HBM per device.

```python
import math
import jax
import jax.numpy as jnp
from jax import lax

SLAB_LAYERS = 8
COLS = 128
PARALLEL_LINES = 256
MERIDIAN_LINES = 2048


def draw_water_indicator(key, part):
    column_depth = jax.random.randint(key, (PARALLEL_LINES, MERIDIAN_LINES), -1, SLAB_LAYERS + 1)
    column_depth = jnp.maximum(column_depth, 0)
    level_index = jnp.arange(SLAB_LAYERS, dtype=jnp.int32)[:, None, None]
    return (level_index < column_depth[None]).astype(jnp.int32)


def draw_seam_mirror_index(key, part):
    tile_count = MERIDIAN_LINES // COLS
    tile_pick = jax.random.randint(jax.random.fold_in(key, 7), (), 0, tile_count)
    fold_pivot = tile_pick * COLS + COLS - 1
    columns = jnp.arange(MERIDIAN_LINES, dtype=jnp.int32)
    return ((fold_pivot - columns) % MERIDIAN_LINES).astype(jnp.int32)


def steps_of(rng, extent, cuts, low, largest):
    gain, own = 1.0, jax.random.fold_in(rng, 6)
    for axis_at, blocks in cuts:
        steps = jnp.exp(jax.random.uniform(jax.random.fold_in(own, axis_at), (blocks,), jnp.float32, low / len(cuts), largest / len(cuts)))
        gain = gain * jnp.repeat(steps, extent[axis_at] // blocks).reshape([-1 if axis == axis_at else 1 for axis in range(len(extent))])
    return gain


def bell_draw(stream_key, shape, scale, most, split=(), kind=jnp.bfloat16):
    drawn = scale * jax.random.normal(stream_key, shape, jnp.float32)
    if split:
        drawn = drawn * steps_of(stream_key, shape, split, -0.22, 0.18)
    return jnp.clip(drawn, -most, most).astype(kind)


def setup_inputs(seed: int = 0) -> dict:
    seeds = jax.random.split(jax.random.key(seed), 11)
    potential_heat = bell_draw(seeds[0], (SLAB_LAYERS, PARALLEL_LINES, MERIDIAN_LINES), 1.0, 6.0, ((1, 2), (2, 16)), jnp.float32)
    saltiness_anomaly = bell_draw(seeds[1], (SLAB_LAYERS, PARALLEL_LINES, MERIDIAN_LINES), 1.0, 6.0, ((1, 2), (2, 16)), jnp.float32)
    east_current = jnp.clip(jax.random.uniform(seeds[2], (SLAB_LAYERS, PARALLEL_LINES, MERIDIAN_LINES), jnp.float32, -1.0, 1.0) * steps_of(seeds[2], (SLAB_LAYERS, PARALLEL_LINES, MERIDIAN_LINES), ((1, 2), (2, 16)), -0.4, 0.0), -1.0, 1.0)
    north_current = jnp.clip(jax.random.uniform(seeds[3], (SLAB_LAYERS, PARALLEL_LINES, MERIDIAN_LINES), jnp.float32, -1.0, 1.0) * steps_of(seeds[3], (SLAB_LAYERS, PARALLEL_LINES, MERIDIAN_LINES), ((1, 2), (2, 16)), -0.4, 0.0), -1.0, 1.0)
    water_indicator = draw_water_indicator(jax.random.fold_in(seeds[10], 71), 0)
    east_west_courant_factor = jnp.clip(jnp.exp(math.log(0.45) - 2.1972245 * jax.random.uniform(seeds[5], (PARALLEL_LINES, MERIDIAN_LINES), jnp.float32) ** steps_of(seeds[5], (PARALLEL_LINES, MERIDIAN_LINES), ((0, 2), (1, 16)), -0.2, 0.2)), 0.05, 0.45)
    north_south_courant_factor = jnp.clip(jnp.exp(math.log(0.45) - 2.1972245 * jax.random.uniform(seeds[6], (PARALLEL_LINES, MERIDIAN_LINES), jnp.float32) ** steps_of(seeds[6], (PARALLEL_LINES, MERIDIAN_LINES), ((0, 2), (1, 16)), -0.2, 0.2)), 0.05, 0.45)
    interface_diffusion_factor = jnp.clip(jnp.exp(math.log(5.0) - 4.6051702 * jax.random.uniform(seeds[7], (SLAB_LAYERS - 1, PARALLEL_LINES, MERIDIAN_LINES), jnp.float32) ** steps_of(seeds[7], (SLAB_LAYERS - 1, PARALLEL_LINES, MERIDIAN_LINES), ((1, 2), (2, 16)), -0.2, 0.2)), 0.05, 5.0)
    spreading_coefficient = jnp.clip(jax.random.uniform(seeds[8], (4, SLAB_LAYERS), jnp.float32, 0.05, 0.25), 0.05, 0.25)
    seam_mirror_index = draw_seam_mirror_index(jax.random.fold_in(seeds[10], 71), 0)
    return dict(potential_heat=potential_heat, saltiness_anomaly=saltiness_anomaly, east_current=east_current, north_current=north_current, water_indicator=water_indicator, east_west_courant_factor=east_west_courant_factor, north_south_courant_factor=north_south_courant_factor, interface_diffusion_factor=interface_diffusion_factor, spreading_coefficient=spreading_coefficient, seam_mirror_index=seam_mirror_index)


def cut(source, first_index, last_index, dimension):
    return lax.slice_in_dim(source, first_index, last_index, axis=dimension)


def ppm_update(extended, courant, opening, dimension):
    length = extended.shape[dimension] - 6
    edge_value = (7.0 / 12.0) * (cut(extended, 1, length + 4, dimension) + cut(extended, 2, length + 5, dimension)) - (1.0 / 12.0) * (cut(extended, 0, length + 3, dimension) + cut(extended, 3, length + 6, dimension))
    left_edge = cut(edge_value, 0, length + 2, dimension)
    right_edge = cut(edge_value, 1, length + 3, dimension)
    centre = cut(extended, 2, length + 4, dimension)
    slopes = right_edge - left_edge
    curvature = 6.0 * (centre - 0.5 * (left_edge + right_edge))
    courant_size = jnp.abs(courant)
    shape_factor = 1.0 - (2.0 / 3.0) * courant_size
    from_left = cut(right_edge, 0, length + 1, dimension) - 0.5 * courant_size * (cut(slopes, 0, length + 1, dimension) - shape_factor * cut(curvature, 0, length + 1, dimension))
    from_right = cut(left_edge, 1, length + 2, dimension) + 0.5 * courant_size * (cut(slopes, 1, length + 2, dimension) + shape_factor * cut(curvature, 1, length + 2, dimension))
    fluxes = courant * opening * jnp.where(courant >= 0.0, from_left, from_right)
    return cut(fluxes, 0, length, dimension) - cut(fluxes, 1, length + 1, dimension)


def face_terms(speed_metric, wet_ext, metric_ext, dimension):
    length = wet_ext.shape[dimension] - 6
    courant = 0.5 * (cut(speed_metric, 2, length + 3, dimension) + cut(speed_metric, 3, length + 4, dimension))
    opening = cut(wet_ext, 2, length + 3, dimension) * cut(wet_ext, 3, length + 4, dimension)
    weight = 0.5 * (cut(metric_ext, 2, length + 3, dimension) + cut(metric_ext, 3, length + 4, dimension)) * opening
    return courant, opening, weight


def vertical_solve(target_rhs, coupling):
    layer_total = target_rhs.shape[1]
    zeros_plane = jnp.zeros_like(target_rhs[:, 0])
    factors = []
    reduced = []
    for layer_index in range(layer_total):
        upward = coupling[layer_index - 1] if layer_index > 0 else zeros_plane
        downward = coupling[layer_index] if layer_index < layer_total - 1 else zeros_plane
        divisor = 1.0 + upward + downward
        target = target_rhs[:, layer_index]
        if layer_index > 0:
            divisor = divisor - upward * factors[layer_index - 1]
            target = target + upward * reduced[layer_index - 1]
        factors.append(downward / divisor)
        reduced.append(target / divisor)
    solved_levels = [reduced[layer_total - 1]]
    for layer_index in range(layer_total - 2, -1, -1):
        solved_levels.insert(0, reduced[layer_index] + factors[layer_index] * solved_levels[0])
    return jnp.stack(solved_levels, axis=1)


def lon_extend(source, width):
    return jnp.concatenate([source[..., -width:], source, source[..., :width]], axis=2)


def lat_extend(source, width, sign_value, seam_mirror_index):
    lower_rows = jnp.zeros_like(source[:, :width, :])
    top_rows = source[:, source.shape[1] - width:, :][:, ::-1, :]
    upper_rows = sign_value * jnp.take(top_rows, seam_mirror_index, axis=2)
    return jnp.concatenate([lower_rows, source, upper_rows], axis=1)


def reference(potential_heat, saltiness_anomaly, east_current, north_current, water_indicator, east_west_courant_factor, north_south_courant_factor, interface_diffusion_factor, spreading_coefficient, seam_mirror_index):
    ocean_point_indicator = water_indicator.astype(jnp.float32)
    transported_quantities = [potential_heat * ocean_point_indicator, saltiness_anomaly * ocean_point_indicator, east_current * ocean_point_indicator, north_current * ocean_point_indicator]
    sign_list = [1.0, 1.0, -1.0, -1.0]
    zonal_row = east_west_courant_factor[None]
    merid_row = north_south_courant_factor[None]
    wet_x = lon_extend(ocean_point_indicator, 3)
    metric_x = lon_extend(zonal_row, 3)
    speed_x = lon_extend(transported_quantities[2], 3) * metric_x
    courant_x, opening_x, weight_x = face_terms(speed_x, wet_x, metric_x, 2)
    starred = [one_field + ppm_update(lon_extend(one_field, 3), courant_x, opening_x, 2) for one_field in transported_quantities]
    wet_y = lat_extend(ocean_point_indicator, 3, 1.0, seam_mirror_index)
    metric_y = lat_extend(merid_row, 3, 1.0, seam_mirror_index)
    speed_y = lat_extend(transported_quantities[3], 3, -1.0, seam_mirror_index) * metric_y
    courant_y, opening_y, weight_y = face_terms(speed_y, wet_y, metric_y, 1)
    advected = [starred[field_index] + ppm_update(lat_extend(starred[field_index], 3, sign_list[field_index], seam_mirror_index), courant_y, opening_y, 1) for field_index in range(4)]
    coupling = interface_diffusion_factor * ocean_point_indicator[:-1] * ocean_point_indicator[1:]
    results = []
    for field_index in range(4):
        one_field = advected[field_index]
        wide_stack = lon_extend(one_field, 1)
        tall_stack = lat_extend(one_field, 1, sign_list[field_index], seam_mirror_index)
        laplacian = weight_x[:, :, 1:] * (wide_stack[:, :, 2:] - one_field) - weight_x[:, :, :-1] * (one_field - wide_stack[:, :, :-2]) + weight_y[:, 1:, :] * (tall_stack[:, 2:, :] - one_field) - weight_y[:, :-1, :] * (one_field - tall_stack[:, :-2, :])
        diffused = one_field + spreading_coefficient[field_index][:, None, None] * laplacian
        solved = vertical_solve(diffused[None], coupling)[0]
        results.append(solved * ocean_point_indicator)
    return (results[0], results[1], results[2], results[3])
```

```python
import jax
import jax.numpy as jnp
from jax import lax
from jax.experimental import pallas as pl
from jax.experimental.pallas import tpu as pltpu
from jax.sharding import PartitionSpec as P

LANES = 128
SP, VM, VMP, WET, WETP, MY, MYP, WX, WXP, PLANES = 32, 34, 42, 43, 51, 52, 53, 54, 62, 63
WIDE, THIN = 34, 20
MSG = WIDE * 4 + THIN * 2
VMEM_LIMIT = 56 * 1024 * 1024


def lane_of(rows):
    return lax.broadcasted_iota(jnp.int32, (rows, LANES), 1)


def roll(x, s):
    if isinstance(s, int):
        s = s % LANES
        if s == 0:
            return x
    return pltpu.roll(x, s, 1)


def shifted(q, halo, s, lane):
    if s > 0:
        return roll(jnp.where(lane < s, halo, q), -s)
    return roll(jnp.where(lane >= LANES + s, halo, q), -s)


def group_roll(x, g):
    return pltpu.roll(x, (LANES - 8 * g) % LANES, 1)


def coefs(courant, opening):
    a = jnp.abs(courant)
    ak = a * (1.0 - (2.0 / 3.0) * a)
    cc = courant * opening
    return (
        cc * (1.0 - 0.5 * a - 1.5 * ak),
        cc * (0.5 * a - 1.5 * ak),
        cc * (3.0 * ak),
        courant >= 0.0,
    )


def edge(qm, q0, q1, q2):
    return (7.0 / 12.0) * (q0 + q1) - (1.0 / 12.0) * (qm + q2)


def flux(cf, em, e0, e1, q0, q1):
    a0, a1, a2, up = cf
    return a0 * e0 + a1 * jnp.where(up, em, e1) + a2 * jnp.where(up, q0, q1)


def pack_kernel(t_ref, s_ref, u_ref, v_ref, wet_ref, mx_ref, my_ref, c_ref):
    rows = 32
    total = t_ref.shape[1]
    lane = lane_of(rows)
    group = ((lane + 4) % LANES) // 8

    def chunk(i, carry):
        r = pl.ds(pl.multiple_of(i * rows, rows), rows)
        wets = [wet_ref[k, r, :].astype(jnp.float32) for k in range(8)]
        for a, pair in enumerate(((t_ref, s_ref), (u_ref, v_ref))):
            acc = jnp.zeros((rows, LANES), jnp.float32)
            for h, ref in enumerate(pair):
                for k in range(8):
                    g = 8 * h + k
                    acc = jnp.where(group == g, roll(ref[k, r, :] * wets[k], 8 * g), acc)
            c_ref[a, r, :] = acc
        acc = jnp.zeros((rows, LANES), jnp.float32)
        for g, x in enumerate(wets + [mx_ref[r, :], my_ref[r, :]]):
            acc = jnp.where(group == g, roll(x, 8 * g), acc)
        c_ref[2, r, :] = acc
        return carry

    lax.fori_loop(0, total // rows, chunk, 0)


def packed_x(c_ref, l_ref, r_ref, T, r, tr, rows):
    lane = lane_of(rows)
    low = lane % 8 < 4
    place = (lane + 4) % LANES
    half = place < 64
    group = place // 8
    parts = []
    for right in (True, False):
        near, far = (c_ref, r_ref) if right else (l_ref, c_ref)
        e = [jnp.where(low, far[a, r, :], near[a, r, :]) for a in range(3)]

        def both(x, first):
            y = pltpu.roll(x, 64, 1)
            return jnp.where(half, x, y) if first else jnp.where(half, y, x)

        def spread(x, g):
            x = jnp.where(group == g, x, 0.0)
            for s in (8, 16, 32, 64):
                x = x + pltpu.roll(x, s, 1)
            return x

        u, v, wet = both(e[1], True), both(e[1], False), both(e[2], True)
        mx, my = spread(e[2], 8), spread(e[2], 9)
        um = u * mx
        opening = wet * roll(wet, -1)
        weight = 0.5 * (mx + roll(mx, -1)) * opening
        cf = coefs(0.5 * (um + roll(um, -1)), opening)
        starred, fluxes = [], []
        for a in range(2):
            q = e[a]
            q1 = roll(q, -1)
            ed = edge(roll(q, 1), q, q1, roll(q, -2))
            f = flux(cf, roll(ed, 1), ed, roll(ed, -1), q, q1)
            starred.append(q + roll(f, 1) - f)
            fluxes.append(f)
        parts.append((starred, fluxes, weight, v * my, wet, my))
    (rs, _, _, rvm, rwet, rmy), (ls, lf, lw, lvm, lwet, lmy) = parts
    for a in range(2):
        T[SP + a, tr, :] = jnp.where(low, rs[a], ls[a])
    T[VMP, tr, :] = jnp.where(low, rvm, lvm)
    T[WETP, tr, :] = jnp.where(low, rwet, lwet)
    T[MYP, tr, :] = jnp.where(low, rmy, lmy)
    T[WXP, tr, :] = lw
    return lf


def x_phase(fields, wet_ref, mx_ref, my_ref, c_ref, l_ref, r_ref, T, H, r, tr, rows):
    lane = lane_of(rows)
    low = lane % 8 < 4
    lf = packed_x(c_ref, l_ref, r_ref, T, r, tr, rows)
    for a in range(3):
        H[a] = jnp.where(low, r_ref[a, r, :], l_ref[a, r, :])
    for a in range(2):
        H[3 + a] = lf[a]
    mx = mx_ref[r, :]
    my = my_ref[r, :]
    T[MY, tr, :] = my
    mxh = group_roll(H[2], 8)
    mx1 = shifted(mx, mxh, 1, lane)

    def level(k, carry):
        wet = wet_ref[k, r, :].astype(jnp.float32)
        T[WET + k, tr, :] = wet
        hwet = group_roll(H[2], k)
        opening = wet * shifted(wet, hwet, 1, lane)
        T[WX + k, tr, :] = 0.5 * (mx + mx1) * opening
        hu = group_roll(H[1], k)
        um = fields[2][k, r, :] * wet * mx
        cf = coefs(0.5 * (um + shifted(um, hu * mxh, 1, lane)), opening)
        for f in range(4):
            q = fields[f][k, r, :] * wet
            if f == 3:
                T[VM + k, tr, :] = q * my
            g = 8 * (f % 2) + k
            h = hu if f == 2 else group_roll(H[f // 2], g)
            qm, q1, q2 = (shifted(q, h, s, lane) for s in (-1, 1, 2))
            ed = edge(qm, q, q1, q2)
            hm1, h1 = roll(h, 1), roll(h, -1)
            m2, p2 = hm1, roll(h, -2)
            em_fix = edge(m2, h, roll(q, -1), roll(q, -2))
            e1_fix = edge(roll(q, 1), h, h1, p2)
            em = roll(jnp.where(lane == LANES - 1, em_fix, ed), 1)
            e1 = roll(jnp.where(lane == 0, e1_fix, ed), -1)
            fl = flux(cf, em, ed, e1, q, q1)
            flm = roll(jnp.where(lane == LANES - 1, group_roll(H[3 + f // 2], g), fl), 1)
            T[8 * f + k, tr, :] = q + flm - fl
        return carry

    lax.fori_loop(0, 8, level, 0)


def face_y(T, vm, wet, my, WY, kw, r0, rows):
    r, r1 = pl.ds(r0, rows), pl.ds(r0 + 1, rows)
    opening = T[wet, r, :] * T[wet, r1, :]
    if WY is not None:
        WY[kw, r, :] = 0.5 * (T[my, r, :] + T[my, r1, :]) * opening
    return coefs(0.5 * (T[vm, r, :] + T[vm, r1, :]), opening)


def y_advect(T, E, F, A, WY, planes, vm, wet, my, kw, chunks):
    for r0, rows in chunks:
        for n, p in enumerate(planes):
            E[n, pl.ds(r0, rows), :] = edge(*(T[p, pl.ds(r0 + s, rows), :] for s in (-1, 0, 1, 2)))
    for r0, rows in chunks:
        cf = face_y(T, vm, wet, my, WY, kw, r0, rows)
        for n, p in enumerate(planes):
            em, e0, e1 = (E[n, pl.ds(r0 + s, rows), :] for s in (-1, 0, 1))
            q0, q1 = (T[p, pl.ds(r0 + s, rows), :] for s in (0, 1))
            F[n, pl.ds(r0, rows), :] = flux(cf, em, e0, e1, q0, q1)
    for r0, rows in chunks:
        for n, p in enumerate(planes):
            r = pl.ds(r0, rows)
            A[p, r, :] = T[p, r, :] + F[n, pl.ds(r0 - 1, rows), :] - F[n, r, :]


def y_phase(T, E, F, A, WY, chunks):
    y_advect(T, E, F, A, None, (SP, SP + 1), VMP, WETP, MYP, 0, chunks)

    def level(k, carry):
        y_advect(T, E, F, A, WY, tuple(8 * f + k for f in range(4)), VM + k, WET + k, MY, k, chunks)
        return carry

    lax.fori_loop(0, 8, level, 0)


def finish(T, A, WY, idf_ref, coef_ref, outs, t0, o0, rows):
    lane = lane_of(rows)
    r, rp, rm = pl.ds(t0, rows), pl.ds(t0 + 1, rows), pl.ds(t0 - 1, rows)
    o = pl.ds(o0, rows)
    wet = [T[WET + k, r, :] for k in range(8)]
    wxp = T[WXP, r, :]
    ap = [A[SP + a, r, :] for a in range(2)]
    up = None
    reduced, factors = [], []
    for k in range(8):
        wx = T[WX + k, r, :]
        wxm = roll(jnp.where(lane == LANES - 1, roll(wxp, -8 * k), wx), 1)
        wy, wym = WY[k, r, :], WY[k, rm, :]
        down = idf_ref[k, o, :] * wet[k] * wet[k + 1] if k < 7 else None
        divisor = 1.0
        if up is not None:
            divisor = divisor + up * (1.0 - factors[-1])
        if down is not None:
            divisor = divisor + down
        inv = 1.0 / divisor
        row = []
        for f in range(4):
            p = 8 * f + k
            a = A[p, r, :]
            h = roll(ap[f // 2], -8 * (8 * (f % 2) + k))
            a1 = roll(jnp.where(lane == 0, h, a), -1)
            am = roll(jnp.where(lane == LANES - 1, h, a), 1)
            lap = wx * (a1 - a) - wxm * (a - am) + wy * (A[p, rp, :] - a) - wym * (a - A[p, rm, :])
            d = a + coef_ref[f, k] * lap
            if up is not None:
                d = d + up * reduced[-1][f]
            row.append(d * inv)
        reduced.append(row)
        if down is not None:
            factors.append(down * inv)
        up = down
    x = reduced[7]
    for k in range(7, -1, -1):
        if k < 7:
            x = [reduced[k][f] + factors[k] * x[f] for f in range(4)]
        for f in range(4):
            outs[f][k, o, :] = x[f] * wet[k]


def edge_rows_kernel(t, s, u, v, wet, mx, my, c, l, r, msg, T, H):
    x_phase((t, s, u, v), wet, mx, my, c, l, r, T, H, pl.ds(0, 8), pl.ds(0, 8), 8)
    side = pl.program_id(0)

    @pl.when(side == 0)
    def _():
        for p in range(WIDE):
            msg[0, 4 * p : 4 * p + 4, :] = T[p, 0:4, :]
        for p in range(THIN):
            msg[0, 4 * WIDE + 2 * p : 4 * WIDE + 2 * p + 2, :] = T[WIDE + p, 0:2, :]

    @pl.when(side == 1)
    def _():
        for p in range(WIDE):
            msg[0, 4 * p : 4 * p + 4, :] = T[p, 4:8, :]
        for p in range(THIN):
            msg[0, 4 * WIDE + 2 * p : 4 * WIDE + 2 * p + 2, :] = T[WIDE + p, 6:8, :]


def interior_kernel(coef, t, s, u, v, wet, mx, my, c, l, r, idf, o0, o1, o2, o3, bnd, T, H, E, F, A, WY):
    total = t.shape[1]
    rows = 32

    def chunk(i, carry):
        a = pl.multiple_of(i * rows, rows)
        x_phase((t, s, u, v), wet, mx, my, c, l, r, T, H, pl.ds(a, rows), pl.ds(pl.multiple_of(a + 8, 8), rows), rows)
        return carry

    lax.fori_loop(0, total // rows, chunk, 0)
    bnd[:, 0:16, :] = T[:, 8:24, :]
    bnd[:, 16:32, :] = T[:, total - 8 : total + 8, :]
    y_phase(T, E, F, A, WY, tuple((8 + i, rows) for i in range(0, total, rows)))

    def tile(i, carry):
        a = pl.multiple_of(i * 8, 8)
        finish(T, A, WY, idf, coef, (o0, o1, o2, o3), a + 8, a, 8)
        return carry

    lax.fori_loop(1, total // 8 - 1, tile, 0)


def border_kernel(place, coef, idf, bnd, from_south, from_north, fold, i0, i1, i2, i3, o0, o1, o2, o3, T, E, F, A, WY, R):
    side = pl.program_id(0)

    @pl.when(side == 0)
    def _():
        T[:, 16:32, :] = bnd[...]
        for p in range(WIDE):
            T[p, 12:16, :] = from_south[4 * p : 4 * p + 4, :]
        for p in range(THIN):
            n = 4 * WIDE + 2 * p
            T[WIDE + p, 14:16, :] = from_south[n : n + 2, :]

    @pl.when(side == 1)
    def _():
        T[:, 8:24, :] = bnd[...]

    @pl.when((side == 1) & (place[1] == 0))
    def _():
        for p in range(WIDE):
            T[p, 24:28, :] = from_north[4 * p : 4 * p + 4, :]
        for p in range(THIN):
            n = 4 * WIDE + 2 * p
            T[WIDE + p, 24:26, :] = from_north[n : n + 2, :]

    @pl.when((side == 1) & (place[1] == 1))
    def _():
        x = fold[0]
        lane = lane_of(MSG)
        row = lax.broadcasted_iota(jnp.int32, (MSG, LANES), 0)
        back = jnp.take_along_axis(x, LANES - 1 - lane, axis=1)
        swap = jnp.where(lane % 8 == 0, roll(x, 1), roll(x, -1))
        w = 4 * WIDE
        packed = (
            ((row >= 4 * SP) & (row < w))
            | ((row >= w + 2 * (VMP - WIDE)) & (row < w + 2 * (WET - WIDE)))
            | ((row >= w + 2 * (WETP - WIDE)) & (row < w + 2 * (MY - WIDE)))
            | (row >= w + 2 * (MYP - WIDE))
        )
        minus = (
            ((row >= 64) & (row < 4 * SP))
            | ((row >= 4 * SP + 4) & (row < w))
            | ((row >= w) & (row < w + 2 * (WET - WIDE)))
        )
        y = jnp.where(packed, swap, back)
        R[...] = jnp.where(minus, -y, y)
        for p in range(WIDE):
            for i in range(4):
                T[p, 24 + i : 25 + i, :] = R[4 * p + 3 - i : 4 * p + 4 - i, :]
        for p in range(THIN):
            for i in range(2):
                n = w + 2 * p + 1 - i
                T[WIDE + p, 24 + i : 25 + i, :] = R[n : n + 1, :]

    y_phase(T, E, F, A, WY, ((8, 24),))
    finish(T, A, WY, idf, coef, (o0, o1, o2, o3), 16, 0, 8)


def vspec():
    return pl.BlockSpec(memory_space=pltpu.VMEM)


def sspec():
    return pl.BlockSpec(memory_space=pltpu.SMEM)


def shards(heat, salt, east, north, water, mx, my, idf, spreading, mirror):
    f32 = jnp.float32
    rows_total = heat.shape[1]
    last = rows_total // 8 - 1
    params = pltpu.CompilerParams(vmem_limit_bytes=VMEM_LIMIT)
    fields = (heat, salt, east, north)
    cols = pl.pallas_call(
        pack_kernel,
        out_shape=jax.ShapeDtypeStruct((3, rows_total, LANES), f32),
        in_specs=[vspec()] * 7,
        out_specs=vspec(),
        compiler_params=params,
    )(*fields, water, mx, my)
    n = lax.axis_size("lon")
    left = lax.ppermute(cols, "lon", [(i, (i + 1) % n) for i in range(n)])
    right = lax.ppermute(cols, "lon", [((i + 1) % n, i) for i in range(n)])

    deep = pl.BlockSpec((8, 8, LANES), lambda i: (0, last * i, 0))
    flat = pl.BlockSpec((8, LANES), lambda i: (last * i, 0))
    three = pl.BlockSpec((3, 8, LANES), lambda i: (0, last * i, 0))
    msg = pl.pallas_call(
        edge_rows_kernel,
        out_shape=jax.ShapeDtypeStruct((2, MSG, LANES), f32),
        grid=(2,),
        in_specs=[deep] * 5 + [flat] * 2 + [three] * 3,
        out_specs=pl.BlockSpec((1, MSG, LANES), lambda i: (i, 0, 0)),
        scratch_shapes=[pltpu.VMEM((PLANES, 8, LANES), f32), pltpu.VMEM((5, 8, LANES), f32)],
        compiler_params=params,
    )(*fields, water, mx, my, cols, left, right)
    m = lax.axis_size("lat")
    from_south = lax.ppermute(msg[1], "lat", [(i, i + 1) for i in range(m - 1)])
    from_north = lax.ppermute(msg[0], "lat", [(i + 1, i) for i in range(m - 1)])
    gathered = lax.all_gather(msg[1], "lon", axis=0)

    tall = rows_total + 16
    out = jax.ShapeDtypeStruct((8, rows_total, LANES), f32)
    results = pl.pallas_call(
        interior_kernel,
        out_shape=[out] * 4 + [jax.ShapeDtypeStruct((PLANES, 32, LANES), f32)],
        in_specs=[sspec()] + [vspec()] * 11,
        out_specs=[vspec()] * 5,
        scratch_shapes=[
            pltpu.VMEM((PLANES, tall, LANES), f32),
            pltpu.VMEM((5, 32, LANES), f32),
            pltpu.VMEM((4, tall, LANES), f32),
            pltpu.VMEM((4, tall, LANES), f32),
            pltpu.VMEM((WIDE, tall, LANES), f32),
            pltpu.VMEM((8, tall, LANES), f32),
        ],
        compiler_params=params,
        cost_estimate=pl.CostEstimate(flops=60_000_000, bytes_accessed=40_000_000, transcendentals=0),
    )(spreading, *fields, water, mx, my, cols, left, right, idf)
    bnd = results[4]

    tile = mirror[0] // LANES
    northern = (lax.axis_index("lat") == m - 1).astype(jnp.int32)
    place = jnp.stack([tile, northern])
    anyspec = pl.BlockSpec(memory_space=pl.ANY)
    whole = pl.BlockSpec((MSG, LANES), lambda i, pf: (0, 0))
    outs = pl.pallas_call(
        border_kernel,
        out_shape=[out] * 4,
        grid_spec=pltpu.PrefetchScalarGridSpec(
            num_scalar_prefetch=1,
            grid=(2,),
            in_specs=[
                sspec(),
                pl.BlockSpec((7, 8, LANES), lambda i, pf: (0, last * i, 0)),
                pl.BlockSpec((PLANES, 16, LANES), lambda i, pf: (0, i, 0)),
                whole,
                whole,
                pl.BlockSpec((1, MSG, LANES), lambda i, pf: (pf[0], 0, 0)),
            ]
            + [anyspec] * 4,
            out_specs=[pl.BlockSpec((8, 8, LANES), lambda i, pf: (0, last * i, 0))] * 4,
            scratch_shapes=[
                pltpu.VMEM((PLANES, 40, LANES), f32),
                pltpu.VMEM((4, 40, LANES), f32),
                pltpu.VMEM((4, 40, LANES), f32),
                pltpu.VMEM((WIDE, 40, LANES), f32),
                pltpu.VMEM((8, 40, LANES), f32),
                pltpu.VMEM((MSG, LANES), f32),
            ],
        ),
        input_output_aliases={7 + i: i for i in range(4)},
        compiler_params=params,
    )(place, spreading, idf, bnd, from_south, from_north, gathered, *results[:4])
    return tuple(outs)


def solution(mesh):
    deep = P(None, "lat", "lon")
    flat = P("lat", "lon")
    return jax.shard_map(
        shards,
        mesh=mesh,
        in_specs=(deep,) * 5 + (flat, flat, deep, P(), P("lon")),
        out_specs=(deep,) * 4,
        check_vma=False,
    )
```

```python
import jax
import jax.numpy as jnp
from jax import lax
from jax.experimental import pallas as pl
from jax.experimental.pallas import tpu as pltpu
from jax.sharding import PartitionSpec as P

LANES = 128
SP, VM, VMP, WET, WETP, MY, MYP, WX, WXP, PLANES = 32, 34, 42, 43, 51, 52, 53, 54, 62, 63
WIDE, THIN = 34, 20
MSG = WIDE * 4 + THIN * 2
VMEM_LIMIT = 56 * 1024 * 1024


def lane_of(rows):
    return lax.broadcasted_iota(jnp.int32, (rows, LANES), 1)


def roll(x, s):
    if isinstance(s, int):
        s = s % LANES
        if s == 0:
            return x
    return pltpu.roll(x, s, 1)


def shifted(q, halo, s, lane):
    if s > 0:
        return roll(jnp.where(lane < s, halo, q), -s)
    return roll(jnp.where(lane >= LANES + s, halo, q), -s)


def group_roll(x, g):
    return roll(x, -8 * g)


def coefs(courant, opening):
    a = jnp.abs(courant)
    ak = a * (1.0 - (2.0 / 3.0) * a)
    cc = courant * opening
    return (
        cc * (1.0 - 0.5 * a - 1.5 * ak),
        cc * (0.5 * a - 1.5 * ak),
        cc * (3.0 * ak),
        courant >= 0.0,
    )


def edge(qm, q0, q1, q2):
    return (7.0 / 12.0) * (q0 + q1) - (1.0 / 12.0) * (qm + q2)


def flux(cf, em, e0, e1, q0, q1):
    a0, a1, a2, up = cf
    return a0 * e0 + a1 * jnp.where(up, em, e1) + a2 * jnp.where(up, q0, q1)


def pack_kernel(t_ref, s_ref, u_ref, v_ref, wet_ref, mx_ref, my_ref, c_ref):
    rows = 32
    total = t_ref.shape[1]
    lane = lane_of(rows)
    group = ((lane + 4) % LANES) // 8

    def chunk(i, carry):
        r = pl.ds(pl.multiple_of(i * rows, rows), rows)
        wets = [wet_ref[k, r, :].astype(jnp.float32) for k in range(8)]
        for a, pair in enumerate(((t_ref, s_ref), (u_ref, v_ref))):
            acc = jnp.zeros((rows, LANES), jnp.float32)
            for h, ref in enumerate(pair):
                for k in range(8):
                    g = 8 * h + k
                    acc = jnp.where(group == g, roll(ref[k, r, :] * wets[k], 8 * g), acc)
            c_ref[a, r, :] = acc
        acc = jnp.zeros((rows, LANES), jnp.float32)
        for g, x in enumerate(wets + [mx_ref[r, :], my_ref[r, :]]):
            acc = jnp.where(group == g, roll(x, 8 * g), acc)
        c_ref[2, r, :] = acc
        return carry

    lax.fori_loop(0, total // rows, chunk, 0)


def packed_x(c_ref, l_ref, r_ref, T, r, tr, rows):
    lane = lane_of(rows)
    low = lane % 8 < 4
    place = (lane + 4) % LANES
    half = place < 64
    group = place // 8
    parts = []
    for right in (True, False):
        near, far = (c_ref, r_ref) if right else (l_ref, c_ref)
        e = [jnp.where(low, far[a, r, :], near[a, r, :]) for a in range(3)]

        def both(x, first):
            y = pltpu.roll(x, 64, 1)
            return jnp.where(half, x, y) if first else jnp.where(half, y, x)

        def spread(x, g):
            x = jnp.where(group == g, x, 0.0)
            for s in (8, 16, 32, 64):
                x = x + pltpu.roll(x, s, 1)
            return x

        u, v, wet = both(e[1], True), both(e[1], False), both(e[2], True)
        mx, my = spread(e[2], 8), spread(e[2], 9)
        um = u * mx
        opening = wet * roll(wet, -1)
        weight = 0.5 * (mx + roll(mx, -1)) * opening
        cf = coefs(0.5 * (um + roll(um, -1)), opening)
        starred, fluxes, edges = [], [], []
        for a in range(2):
            q = e[a]
            q1 = roll(q, -1)
            ed = edge(roll(q, 1), q, q1, roll(q, -2))
            f = flux(cf, roll(ed, 1), ed, roll(ed, -1), q, q1)
            starred.append(q + roll(f, 1) - f)
            fluxes.append(f)
            edges.append(ed)
        parts.append((starred, fluxes, edges, weight, v * my, wet, my))
    (rs, _, re, _, rvm, rwet, rmy), (ls, lf, le, lw, lvm, lwet, lmy) = parts
    for a in range(2):
        T[SP + a, tr, :] = jnp.where(low, rs[a], ls[a])
    T[VMP, tr, :] = jnp.where(low, rvm, lvm)
    T[WETP, tr, :] = jnp.where(low, rwet, lwet)
    T[MYP, tr, :] = jnp.where(low, rmy, lmy)
    T[WXP, tr, :] = lw
    return lf, [jnp.where(low, re[a], le[a]) for a in range(2)]


def x_phase(fields, wet_ref, mx_ref, my_ref, c_ref, l_ref, r_ref, T, H, r, tr, rows):
    lane = lane_of(rows)
    low = lane % 8 < 4
    lf, le = packed_x(c_ref, l_ref, r_ref, T, r, tr, rows)
    for a in range(3):
        H[a] = jnp.where(low, r_ref[a, r, :], l_ref[a, r, :])
    for a in range(2):
        H[3 + a] = lf[a]
        H[5 + a] = le[a]
    mx = mx_ref[r, :]
    my = my_ref[r, :]
    T[MY, tr, :] = my
    mxh = group_roll(H[2], 8)
    mx1 = shifted(mx, mxh, 1, lane)

    def level(k, carry):
        wet = wet_ref[k, r, :].astype(jnp.float32)
        T[WET + k, tr, :] = wet
        hwet = group_roll(H[2], k)
        opening = wet * shifted(wet, hwet, 1, lane)
        T[WX + k, tr, :] = 0.5 * (mx + mx1) * opening
        hu = group_roll(H[1], k)
        um = fields[2][k, r, :] * wet * mx
        cf = coefs(0.5 * (um + shifted(um, hu * mxh, 1, lane)), opening)
        for f in range(4):
            q = fields[f][k, r, :] * wet
            if f == 3:
                T[VM + k, tr, :] = q * my
            g = 8 * (f % 2) + k
            h = hu if f == 2 else group_roll(H[f // 2], g)
            qm, q1, q2 = (shifted(q, h, s, lane) for s in (-1, 1, 2))
            ed = edge(qm, q, q1, q2)
            he = group_roll(H[5 + f // 2], g)
            em = roll(jnp.where(lane == LANES - 1, he, ed), 1)
            e1 = roll(jnp.where(lane == 0, he, ed), -1)
            fl = flux(cf, em, ed, e1, q, q1)
            flm = roll(jnp.where(lane == LANES - 1, group_roll(H[3 + f // 2], g), fl), 1)
            T[8 * f + k, tr, :] = q + flm - fl

    for k in range(8):
        level(k, 0)


def face_y(T, vm, wet, my, WY, kw, r0, rows):
    r, r1 = pl.ds(r0, rows), pl.ds(r0 + 1, rows)
    opening = T[wet, r, :] * T[wet, r1, :]
    if WY is not None:
        WY[kw, r, :] = 0.5 * (T[my, r, :] + T[my, r1, :]) * opening
    return coefs(0.5 * (T[vm, r, :] + T[vm, r1, :]), opening)


def y_advect(T, E, F, A, WY, planes, vm, wet, my, kw, chunks):
    for r0, rows in chunks:
        for n, p in enumerate(planes):
            E[n, pl.ds(r0, rows), :] = edge(*(T[p, pl.ds(r0 + s, rows), :] for s in (-1, 0, 1, 2)))
    for r0, rows in chunks:
        cf = face_y(T, vm, wet, my, WY, kw, r0, rows)
        for n, p in enumerate(planes):
            em, e0, e1 = (E[n, pl.ds(r0 + s, rows), :] for s in (-1, 0, 1))
            q0, q1 = (T[p, pl.ds(r0 + s, rows), :] for s in (0, 1))
            F[n, pl.ds(r0, rows), :] = flux(cf, em, e0, e1, q0, q1)
    for r0, rows in chunks:
        for n, p in enumerate(planes):
            r = pl.ds(r0, rows)
            A[p, r, :] = T[p, r, :] + F[n, pl.ds(r0 - 1, rows), :] - F[n, r, :]


def y_phase(T, E, F, A, WY, chunks):
    y_advect(T, E, F, A, None, (SP, SP + 1), VMP, WETP, MYP, 0, chunks)

    for k in range(8):
        y_advect(T, E, F, A, WY, tuple(8 * f + k for f in range(4)), VM + k, WET + k, MY, k, chunks)


def finish(T, A, WY, idf_ref, coef_ref, outs, t0, o0, rows):
    lane = lane_of(rows)
    r, rp, rm = pl.ds(t0, rows), pl.ds(t0 + 1, rows), pl.ds(t0 - 1, rows)
    o = pl.ds(o0, rows)
    wet = [T[WET + k, r, :] for k in range(8)]
    wxp = T[WXP, r, :]
    ap = [A[SP + a, r, :] for a in range(2)]
    up = None
    reduced, factors = [], []
    for k in range(8):
        wx = T[WX + k, r, :]
        wxm = roll(jnp.where(lane == LANES - 1, roll(wxp, -8 * k), wx), 1)
        wy, wym = WY[k, r, :], WY[k, rm, :]
        down = idf_ref[k, o, :] * wet[k] * wet[k + 1] if k < 7 else None
        divisor = 1.0
        if up is not None:
            divisor = divisor + up * (1.0 - factors[-1])
        if down is not None:
            divisor = divisor + down
        inv = 1.0 / divisor
        row = []
        for f in range(4):
            p = 8 * f + k
            a = A[p, r, :]
            h = roll(ap[f // 2], -8 * (8 * (f % 2) + k))
            a1 = roll(jnp.where(lane == 0, h, a), -1)
            am = roll(jnp.where(lane == LANES - 1, h, a), 1)
            lap = wx * (a1 - a) - wxm * (a - am) + wy * (A[p, rp, :] - a) - wym * (a - A[p, rm, :])
            d = a + coef_ref[f, k] * lap
            if up is not None:
                d = d + up * reduced[-1][f]
            row.append(d * inv)
        reduced.append(row)
        if down is not None:
            factors.append(down * inv)
        up = down
    x = reduced[7]
    for k in range(7, -1, -1):
        if k < 7:
            x = [reduced[k][f] + factors[k] * x[f] for f in range(4)]
        for f in range(4):
            outs[f][k, o, :] = x[f] * wet[k]


def edge_rows_kernel(t, s, u, v, wet, mx, my, c, l, r, msg, T, H):
    x_phase((t, s, u, v), wet, mx, my, c, l, r, T, H, pl.ds(0, 8), pl.ds(0, 8), 8)
    side = pl.program_id(0)

    @pl.when(side == 0)
    def _():
        for p in range(WIDE):
            msg[0, 4 * p : 4 * p + 4, :] = T[p, 0:4, :]
        for p in range(THIN):
            msg[0, 4 * WIDE + 2 * p : 4 * WIDE + 2 * p + 2, :] = T[WIDE + p, 0:2, :]

    @pl.when(side == 1)
    def _():
        for p in range(WIDE):
            msg[0, 4 * p : 4 * p + 4, :] = T[p, 4:8, :]
        for p in range(THIN):
            msg[0, 4 * WIDE + 2 * p : 4 * WIDE + 2 * p + 2, :] = T[WIDE + p, 6:8, :]


def interior_kernel(coef, t, s, u, v, wet, mx, my, c, l, r, idf, o0, o1, o2, o3, bnd, T, H, E, F, A, WY):
    total = t.shape[1]
    rows = 32
    step = 16

    def chunk(i, carry):
        a = pl.multiple_of(i * step, step)
        x_phase((t, s, u, v), wet, mx, my, c, l, r, T, H, pl.ds(a, step), pl.ds(pl.multiple_of(a + 8, 8), step), step)
        return carry

    lax.fori_loop(0, total // step, chunk, 0)
    bnd[:, 0:16, :] = T[:, 8:24, :]
    bnd[:, 16:32, :] = T[:, total - 8 : total + 8, :]
    y_phase(T, E, F, A, WY, tuple((8 + i, rows) for i in range(0, total, rows)))

    def tile(i, carry):
        a = pl.multiple_of(i * 8, 8)
        finish(T, A, WY, idf, coef, (o0, o1, o2, o3), a + 8, a, 8)
        return carry

    lax.fori_loop(1, total // 8 - 1, tile, 0)


def border_kernel(place, coef, idf, bnd, from_south, from_north, fold, i0, i1, i2, i3, o0, o1, o2, o3, T, E, F, A, WY, R):
    side = pl.program_id(0)

    @pl.when(side == 0)
    def _():
        T[:, 16:32, :] = bnd[...]
        for p in range(WIDE):
            T[p, 12:16, :] = from_south[4 * p : 4 * p + 4, :]
        for p in range(THIN):
            n = 4 * WIDE + 2 * p
            T[WIDE + p, 14:16, :] = from_south[n : n + 2, :]

    @pl.when(side == 1)
    def _():
        T[:, 8:24, :] = bnd[...]

    @pl.when((side == 1) & (place[1] == 0))
    def _():
        for p in range(WIDE):
            T[p, 24:28, :] = from_north[4 * p : 4 * p + 4, :]
        for p in range(THIN):
            n = 4 * WIDE + 2 * p
            T[WIDE + p, 24:26, :] = from_north[n : n + 2, :]

    @pl.when((side == 1) & (place[1] == 1))
    def _():
        x = fold[0]
        lane = lane_of(MSG)
        row = lax.broadcasted_iota(jnp.int32, (MSG, LANES), 0)
        back = jnp.take_along_axis(x, LANES - 1 - lane, axis=1)
        swap = jnp.where(lane % 8 == 0, roll(x, 1), roll(x, -1))
        w = 4 * WIDE
        packed = (
            ((row >= 4 * SP) & (row < w))
            | ((row >= w + 2 * (VMP - WIDE)) & (row < w + 2 * (WET - WIDE)))
            | ((row >= w + 2 * (WETP - WIDE)) & (row < w + 2 * (MY - WIDE)))
            | (row >= w + 2 * (MYP - WIDE))
        )
        minus = (
            ((row >= 64) & (row < 4 * SP))
            | ((row >= 4 * SP + 4) & (row < w))
            | ((row >= w) & (row < w + 2 * (WET - WIDE)))
        )
        y = jnp.where(packed, swap, back)
        R[...] = jnp.where(minus, -y, y)
        for p in range(WIDE):
            for i in range(4):
                T[p, 24 + i : 25 + i, :] = R[4 * p + 3 - i : 4 * p + 4 - i, :]
        for p in range(THIN):
            for i in range(2):
                n = w + 2 * p + 1 - i
                T[WIDE + p, 24 + i : 25 + i, :] = R[n : n + 1, :]

    y_phase(T, E, F, A, WY, ((8, 24),))
    finish(T, A, WY, idf, coef, (o0, o1, o2, o3), 16, 0, 8)


def vspec():
    return pl.BlockSpec(memory_space=pltpu.VMEM)


def sspec():
    return pl.BlockSpec(memory_space=pltpu.SMEM)


def shards(heat, salt, east, north, water, mx, my, idf, spreading, mirror):
    f32 = jnp.float32
    rows_total = heat.shape[1]
    last = rows_total // 8 - 1
    params = pltpu.CompilerParams(vmem_limit_bytes=VMEM_LIMIT)
    fields = (heat, salt, east, north)
    cols = pl.pallas_call(
        pack_kernel,
        out_shape=jax.ShapeDtypeStruct((3, rows_total, LANES), f32),
        in_specs=[vspec()] * 7,
        out_specs=vspec(),
        compiler_params=params,
    )(*fields, water, mx, my)
    n = lax.axis_size("lon")
    left = lax.ppermute(cols, "lon", [(i, (i + 1) % n) for i in range(n)])
    right = lax.ppermute(cols, "lon", [((i + 1) % n, i) for i in range(n)])

    deep = pl.BlockSpec((8, 8, LANES), lambda i: (0, last * i, 0))
    flat = pl.BlockSpec((8, LANES), lambda i: (last * i, 0))
    three = pl.BlockSpec((3, 8, LANES), lambda i: (0, last * i, 0))
    msg = pl.pallas_call(
        edge_rows_kernel,
        out_shape=jax.ShapeDtypeStruct((2, MSG, LANES), f32),
        grid=(2,),
        in_specs=[deep] * 5 + [flat] * 2 + [three] * 3,
        out_specs=pl.BlockSpec((1, MSG, LANES), lambda i: (i, 0, 0)),
        scratch_shapes=[pltpu.VMEM((PLANES, 8, LANES), f32), pltpu.VMEM((7, 8, LANES), f32)],
        compiler_params=params,
    )(*fields, water, mx, my, cols, left, right)
    m = lax.axis_size("lat")
    from_south = lax.ppermute(msg[1], "lat", [(i, i + 1) for i in range(m - 1)])
    from_north = lax.ppermute(msg[0], "lat", [(i + 1, i) for i in range(m - 1)])
    gathered = lax.all_gather(msg[1], "lon", axis=0)

    tall = rows_total + 16
    out = jax.ShapeDtypeStruct((8, rows_total, LANES), f32)
    results = pl.pallas_call(
        interior_kernel,
        out_shape=[out] * 4 + [jax.ShapeDtypeStruct((PLANES, 32, LANES), f32)],
        in_specs=[sspec()] + [vspec()] * 11,
        out_specs=[vspec()] * 5,
        scratch_shapes=[
            pltpu.VMEM((PLANES, tall, LANES), f32),
            pltpu.VMEM((7, 16, LANES), f32),
            pltpu.VMEM((4, tall, LANES), f32),
            pltpu.VMEM((4, tall, LANES), f32),
            pltpu.VMEM((WIDE, tall, LANES), f32),
            pltpu.VMEM((8, tall, LANES), f32),
        ],
        compiler_params=params,
        cost_estimate=pl.CostEstimate(flops=60_000_000, bytes_accessed=40_000_000, transcendentals=0),
    )(spreading, *fields, water, mx, my, cols, left, right, idf)
    bnd = results[4]

    tile = mirror[0] // LANES
    northern = (lax.axis_index("lat") == m - 1).astype(jnp.int32)
    place = jnp.stack([tile, northern])
    anyspec = pl.BlockSpec(memory_space=pl.ANY)
    whole = pl.BlockSpec((MSG, LANES), lambda i, pf: (0, 0))
    outs = pl.pallas_call(
        border_kernel,
        out_shape=[out] * 4,
        grid_spec=pltpu.PrefetchScalarGridSpec(
            num_scalar_prefetch=1,
            grid=(2,),
            in_specs=[
                sspec(),
                pl.BlockSpec((7, 8, LANES), lambda i, pf: (0, last * i, 0)),
                pl.BlockSpec((PLANES, 16, LANES), lambda i, pf: (0, i, 0)),
                whole,
                whole,
                pl.BlockSpec((1, MSG, LANES), lambda i, pf: (pf[0], 0, 0)),
            ]
            + [anyspec] * 4,
            out_specs=[pl.BlockSpec((8, 8, LANES), lambda i, pf: (0, last * i, 0))] * 4,
            scratch_shapes=[
                pltpu.VMEM((PLANES, 40, LANES), f32),
                pltpu.VMEM((4, 40, LANES), f32),
                pltpu.VMEM((4, 40, LANES), f32),
                pltpu.VMEM((WIDE, 40, LANES), f32),
                pltpu.VMEM((8, 40, LANES), f32),
                pltpu.VMEM((MSG, LANES), f32),
            ],
        ),
        input_output_aliases={7 + i: i for i in range(4)},
        compiler_params=params,
    )(place, spreading, idf, bnd, from_south, from_north, gathered, *results[:4])
    return tuple(outs)


def solution(mesh):
    deep = P(None, "lat", "lon")
    flat = P("lat", "lon")
    return jax.shard_map(
        shards,
        mesh=mesh,
        in_specs=(deep,) * 5 + (flat, flat, deep, P(), P("lon")),
        out_specs=(deep,) * 4,
        check_vma=False,
    )
```

```python
import functools

import jax
import jax.numpy as jnp
from jax import lax
from jax.experimental import pallas as pl
from jax.experimental.pallas import tpu as pltpu
from jax.sharding import PartitionSpec as P

LANES = 128
SP, VM, VMP, WET, WETP, MY, MYP, WX, WXP, PLANES = 32, 34, 42, 43, 51, 52, 53, 54, 62, 63
WIDE, THIN = 34, 20
MSG = WIDE * 4 + THIN * 2
VMEM_LIMIT = 56 * 1024 * 1024


def lane_of(rows):
    return lax.broadcasted_iota(jnp.int32, (rows, LANES), 1)


def roll(x, s):
    if isinstance(s, int):
        s = s % LANES
        if s == 0:
            return x
    return pltpu.roll(x, s, 1)


def shifted(q, halo, s, lane):
    if s > 0:
        return roll(jnp.where(lane < s, halo, q), -s)
    return roll(jnp.where(lane >= LANES + s, halo, q), -s)


def group_roll(x, g):
    return pltpu.roll(x, (LANES - 8 * g) % LANES, 1)


def coefs(courant, opening):
    a = jnp.abs(courant)
    ak = a * (1.0 - (2.0 / 3.0) * a)
    cc = courant * opening
    return (
        cc * (1.0 - 0.5 * a - 1.5 * ak),
        cc * (0.5 * a - 1.5 * ak),
        cc * (3.0 * ak),
        courant >= 0.0,
    )


def edge(qm, q0, q1, q2):
    return (7.0 / 12.0) * (q0 + q1) - (1.0 / 12.0) * (qm + q2)


def flux(cf, em, e0, e1, q0, q1):
    a0, a1, a2, up = cf
    return a0 * e0 + a1 * jnp.where(up, em, e1) + a2 * jnp.where(up, q0, q1)


def pack_array(a, refs, wet_ref, mx_ref, my_ref, c_ref):
    rows = 32
    total = c_ref.shape[1]
    lane = lane_of(rows)
    group = ((lane + 4) % LANES) // 8

    def chunk(i, carry):
        r = pl.ds(pl.multiple_of(i * rows, rows), rows)
        wets = [wet_ref[k, r, :].astype(jnp.float32) for k in range(8)]
        acc = jnp.zeros((rows, LANES), jnp.float32)
        if a < 2:
            items = [refs[2 * a + h][k, r, :] * wets[k] for h in range(2) for k in range(8)]
        else:
            items = wets + [mx_ref[r, :], my_ref[r, :]]
        for g, x in enumerate(items):
            acc = jnp.where(group == g, roll(x, 8 * g), acc)
        c_ref[a, r, :] = acc
        return carry

    lax.fori_loop(0, total // rows, chunk, 0)


def packed_x(c_ref, l_ref, r_ref, T, get, tr, rows):
    lane = lane_of(rows)
    low = lane % 8 < 4
    place = (lane + 4) % LANES
    half = place < 64
    group = place // 8
    parts = []
    for right in (True, False):
        near, far = (c_ref, r_ref) if right else (l_ref, c_ref)
        e = [jnp.where(low, get(far, a), get(near, a)) for a in range(3)]

        def both(x, first):
            y = pltpu.roll(x, 64, 1)
            return jnp.where(half, x, y) if first else jnp.where(half, y, x)

        def spread(x, g):
            x = jnp.where(group == g, x, 0.0)
            for s in (8, 16, 32, 64):
                x = x + pltpu.roll(x, s, 1)
            return x

        u, v, wet = both(e[1], True), both(e[1], False), both(e[2], True)
        mx, my = spread(e[2], 8), spread(e[2], 9)
        um = u * mx
        opening = wet * roll(wet, -1)
        weight = 0.5 * (mx + roll(mx, -1)) * opening
        cf = coefs(0.5 * (um + roll(um, -1)), opening)
        starred, fluxes, edges = [], [], []
        for a in range(2):
            q = e[a]
            q1 = roll(q, -1)
            ed = edge(roll(q, 1), q, q1, roll(q, -2))
            f = flux(cf, roll(ed, 1), ed, roll(ed, -1), q, q1)
            starred.append(q + roll(f, 1) - f)
            fluxes.append(f)
            edges.append(ed)
        parts.append((starred, fluxes, edges, weight, v * my, wet, my))
    (rs, _, re, _, rvm, rwet, rmy), (ls, lf, le, lw, lvm, lwet, lmy) = parts
    for a in range(2):
        T[SP + a, tr, :] = jnp.where(low, rs[a], ls[a])
    T[VMP, tr, :] = jnp.where(low, rvm, lvm)
    T[WETP, tr, :] = jnp.where(low, rwet, lwet)
    T[MYP, tr, :] = jnp.where(low, rmy, lmy)
    T[WXP, tr, :] = lw
    return lf, [jnp.where(low, re[a], le[a]) for a in range(2)]


def x_phase(fields, wet_ref, mx_ref, my_ref, c_ref, l_ref, r_ref, T, H, get, tr, rows, unroll):
    lane = lane_of(rows)
    low = lane % 8 < 4
    lf, le = packed_x(c_ref, l_ref, r_ref, T, get, tr, rows)
    for a in range(3):
        H[a] = jnp.where(low, get(r_ref, a), get(l_ref, a))
    for a in range(2):
        H[3 + a] = lf[a]
        H[5 + a] = le[a]
    mx = get(mx_ref)
    my = get(my_ref)
    T[MY, tr, :] = my
    mxh = group_roll(H[2], 8)
    mx1 = shifted(mx, mxh, 1, lane)

    def level(k, carry):
        wet = get(wet_ref, k).astype(jnp.float32)
        T[WET + k, tr, :] = wet
        hwet = group_roll(H[2], k)
        opening = wet * shifted(wet, hwet, 1, lane)
        T[WX + k, tr, :] = 0.5 * (mx + mx1) * opening
        hu = group_roll(H[1], k)
        um = get(fields[2], k) * wet * mx
        cf = coefs(0.5 * (um + shifted(um, hu * mxh, 1, lane)), opening)
        for f in range(4):
            q = get(fields[f], k) * wet
            if f == 3:
                T[VM + k, tr, :] = q * my
            g = 8 * (f % 2) + k
            h = hu if f == 2 else group_roll(H[f // 2], g)
            qm, q1, q2 = (shifted(q, h, s, lane) for s in (-1, 1, 2))
            ed = edge(qm, q, q1, q2)
            he = group_roll(H[5 + f // 2], g)
            em = roll(jnp.where(lane == LANES - 1, he, ed), 1)
            e1 = roll(jnp.where(lane == 0, he, ed), -1)
            fl = flux(cf, em, ed, e1, q, q1)
            flm = roll(jnp.where(lane == LANES - 1, group_roll(H[3 + f // 2], g), fl), 1)
            T[8 * f + k, tr, :] = q + flm - fl

    def levels(i, carry):
        for j in range(unroll):
            level(i * unroll + j, 0)
        return carry

    lax.fori_loop(0, 8 // unroll, levels, 0)


def face_y(T, vm, wet, my, WY, kw, r0, rows):
    r, r1 = pl.ds(r0, rows), pl.ds(r0 + 1, rows)
    opening = T[wet, r, :] * T[wet, r1, :]
    if WY is not None:
        WY[kw, r, :] = 0.5 * (T[my, r, :] + T[my, r1, :]) * opening
    return coefs(0.5 * (T[vm, r, :] + T[vm, r1, :]), opening)


def y_advect(T, E, F, A, WY, planes, vm, wet, my, kw, chunks):
    for r0, rows in chunks:
        for n, p in enumerate(planes):
            E[n, pl.ds(r0, rows), :] = edge(*(T[p, pl.ds(r0 + s, rows), :] for s in (-1, 0, 1, 2)))
    for r0, rows in chunks:
        cf = face_y(T, vm, wet, my, WY, kw, r0, rows)
        for n, p in enumerate(planes):
            em, e0, e1 = (E[n, pl.ds(r0 + s, rows), :] for s in (-1, 0, 1))
            q0, q1 = (T[p, pl.ds(r0 + s, rows), :] for s in (0, 1))
            F[n, pl.ds(r0, rows), :] = flux(cf, em, e0, e1, q0, q1)
    for r0, rows in chunks:
        for n, p in enumerate(planes):
            r = pl.ds(r0, rows)
            A[p, r, :] = T[p, r, :] + F[n, pl.ds(r0 - 1, rows), :] - F[n, r, :]


def y_phase(T, E, F, A, WY, chunks):
    y_advect(T, E, F, A, None, (SP, SP + 1), VMP, WETP, MYP, 0, chunks)

    def level(k, carry):
        y_advect(T, E, F, A, WY, tuple(8 * f + k for f in range(4)), VM + k, WET + k, MY, k, chunks)
        return carry

    lax.fori_loop(0, 8, level, 0)


def factorize(T, idf_ref, U, INV, FAC, base, rows):
    r = pl.ds(base, rows)
    wet = T[WET, r, :]
    up, factor = None, None
    for k in range(8):
        divisor = 1.0
        if k > 0:
            divisor = divisor + up * (1.0 - factor)
        if k < 7:
            below = T[WET + k + 1, r, :]
            down = idf_ref[k] * wet * below
            wet = below
            U[k] = down
            divisor = divisor + down
        inv = 1.0 / divisor
        INV[k] = inv
        if k < 7:
            factor = down * inv
            FAC[k] = factor
            up = down


def finish(T, A, WY, U, INV, FAC, coef_ref, outs, t0, o0, rows):
    lane = lane_of(rows)
    r, rp, rm = pl.ds(t0, rows), pl.ds(t0 + 1, rows), pl.ds(t0 - 1, rows)
    o = pl.ds(o0, rows)
    wxp = T[WXP, r, :]
    ap = [A[SP + a, r, :] for a in range(2)]
    reduced = []
    for k in range(8):
        wx = T[WX + k, r, :]
        wxm = roll(jnp.where(lane == LANES - 1, roll(wxp, -8 * k), wx), 1)
        wy, wym = WY[k, r, :], WY[k, rm, :]
        inv = INV[k, o, :]
        row = []
        for f in range(4):
            p = 8 * f + k
            a = A[p, r, :]
            h = roll(ap[f // 2], -8 * (8 * (f % 2) + k))
            a1 = roll(jnp.where(lane == 0, h, a), -1)
            am = roll(jnp.where(lane == LANES - 1, h, a), 1)
            lap = wx * (a1 - a) - wxm * (a - am) + wy * (A[p, rp, :] - a) - wym * (a - A[p, rm, :])
            d = a + coef_ref[f, k] * lap
            if k > 0:
                d = d + U[k - 1, o, :] * reduced[-1][f]
            row.append(d * inv)
        reduced.append(row)
    x = reduced[7]
    for k in range(7, -1, -1):
        if k < 7:
            factor = FAC[k, o, :]
            x = [reduced[k][f] + factor * x[f] for f in range(4)]
        wet = T[WET + k, r, :]
        for f in range(4):
            outs[f][k, o, :] = x[f] * wet


LOW = 4
MESH = pl.DeviceIdType.MESH


def halo_kernel(
    lon_n, lat_n, tile, t, s, u, v, wet, mx, my, c_out, l_out, r_out, south, north,
    C, L, R, T, H, Mn, Ms, FS, FN, RA, RB, back,
    s_lon, r_lon, s_lat, r_lat, s_a, r_a, s_b, r_b,
):
    total = t.shape[1]
    me = lax.axis_index("lon")
    lat = lax.axis_index("lat")
    right, left = lax.rem(me + 1, lon_n), lax.rem(me + lon_n - 1, lon_n)
    low, high = lax.rem(me, LOW), me // LOW
    layers = lon_n // LOW
    first, last = lat == 0, lat == lat_n - 1
    ring = [left, right]
    ring += [high * LOW + lax.rem(low + d, LOW) for d in range(1, LOW)]
    ring += [lax.rem(high + d, layers) * LOW + low for d in range(1, layers)]
    barrier = pltpu.get_barrier_semaphore()
    for other in ring:
        pl.semaphore_signal(barrier, inc=1, device_id={"lon": other}, device_id_type=MESH)

    @pl.when(jnp.logical_not(first))
    def _():
        pl.semaphore_signal(barrier, inc=1, device_id={"lat": lat - 1}, device_id_type=MESH)

    @pl.when(jnp.logical_not(last))
    def _():
        pl.semaphore_signal(barrier, inc=1, device_id={"lat": lat + 1}, device_id_type=MESH)

    def send(src, dst, ss, rs, where):
        return pltpu.make_async_remote_copy(
            src_ref=src, dst_ref=dst, send_sem=ss, recv_sem=rs, device_id=where, device_id_type=MESH
        )

    fields = (t, s, u, v)
    lon_copies = []
    for a in range(3):
        pack_array(a, fields, wet, mx, my, C)
        if a == 0:
            peers = len(ring) + jnp.where(first, 0, 1) + jnp.where(last, 0, 1)
            pl.semaphore_wait(barrier, peers)
        for dst, where, i in ((R, left, 0), (L, right, 1)):
            cp = send(C.at[a], dst.at[a], s_lon.at[2 * a + i], r_lon.at[2 * a + i], {"lon": where})
            cp.start()
            lon_copies.append(cp)
    for cp in lon_copies:
        cp.wait()

    def get(ref, *k):
        return jnp.concatenate([ref[(*k, pl.ds(0, 8))], ref[(*k, pl.ds(total - 8, 8))]], axis=0)

    x_phase(fields, wet, mx, my, C, L, R, T, H, get, pl.ds(0, 16), 16, 4)
    for p in range(WIDE):
        Mn[4 * p : 4 * p + 4, :] = T[p, 12:16, :]
    for p in range(THIN):
        n = 4 * WIDE + 2 * p
        Mn[n : n + 2, :] = T[WIDE + p, 14:16, :]
    a_copies = []
    for d in range(1, LOW):
        cp = send(Mn, RA.at[low], s_a.at[d], r_a.at[d], {"lon": high * LOW + lax.rem(low + d, LOW)})
        cp.start()
        a_copies.append(cp)
    to_north = send(Mn, FS, s_lat.at[0], r_lat.at[0], {"lat": lat + 1})
    to_south = send(Ms, FN, s_lat.at[1], r_lat.at[1], {"lat": lat - 1})

    @pl.when(jnp.logical_not(last))
    def _():
        to_north.start()

    for p in range(WIDE):
        Ms[4 * p : 4 * p + 4, :] = T[p, 0:4, :]
    for p in range(THIN):
        n = 4 * WIDE + 2 * p
        Ms[n : n + 2, :] = T[WIDE + p, 0:2, :]

    @pl.when(jnp.logical_not(first))
    def _():
        to_south.start()

    RA[low] = Mn[...]
    for a in range(3):
        c_out[a] = C[a]
        l_out[a] = L[a]
        r_out[a] = R[a]
    for cp in a_copies:
        cp.wait()
    RB[high] = RA[lax.rem(tile[0], LOW)]
    b_copies = []
    for d in range(1, layers):
        cp = send(RB.at[high], RB.at[high], s_b.at[d], r_b.at[d], {"lon": lax.rem(high + d, layers) * LOW + low})
        cp.start()
        b_copies.append(cp)

    @pl.when(jnp.logical_not(last))
    def _():
        to_north.wait_send()
        to_south.wait_recv()
        north[...] = FN[...]

    @pl.when(jnp.logical_not(first))
    def _():
        to_south.wait_send()
        to_north.wait_recv()
        south[...] = FS[...]

    @pl.when(first)
    def _():
        south[...] = jnp.zeros((MSG, LANES), jnp.float32)

    for cp in b_copies:
        cp.wait()

    @pl.when(last)
    def _():
        x = RB[tile[0] // LOW]
        lane = lane_of(MSG)
        row = lax.broadcasted_iota(jnp.int32, (MSG, LANES), 0)
        flip = jnp.take_along_axis(x, LANES - 1 - lane, axis=1)
        swap = jnp.where(lane % 8 == 0, roll(x, 1), roll(x, -1))
        w = 4 * WIDE
        packed = (
            ((row >= 4 * SP) & (row < w))
            | ((row >= w + 2 * (VMP - WIDE)) & (row < w + 2 * (WET - WIDE)))
            | ((row >= w + 2 * (WETP - WIDE)) & (row < w + 2 * (MY - WIDE)))
            | (row >= w + 2 * (MYP - WIDE))
        )
        minus = (
            ((row >= 64) & (row < 4 * SP))
            | ((row >= 4 * SP + 4) & (row < w))
            | ((row >= w) & (row < w + 2 * (WET - WIDE)))
        )
        y = jnp.where(packed, swap, flip)
        back[...] = jnp.where(minus, -y, y)
        for p in range(WIDE):
            for i in range(4):
                north[4 * p + i : 4 * p + i + 1, :] = back[4 * p + 3 - i : 4 * p + 4 - i, :]
        for p in range(THIN):
            n = w + 2 * p
            for i in range(2):
                north[n + i : n + i + 1, :] = back[n + 1 - i : n + 2 - i, :]


BASE = 16


def step_kernel(
    coef, t, s, u, v, wet, mx, my, c, l, r, south, north, idf, o0, o1, o2, o3, T, H, E, F, A, WY, U, INV, FAC
):
    total = t.shape[1]

    def get(ref, *k):
        return ref[k] if k else ref[...]

    x_phase((t, s, u, v), wet, mx, my, c, l, r, T, H, get, pl.ds(BASE, total), total, 1)
    factorize(T, idf, U, INV, FAC, BASE, total)
    top = BASE + total
    for p in range(WIDE):
        T[p, BASE - 4 : BASE, :] = south[4 * p : 4 * p + 4, :]
        T[p, top : top + 4, :] = north[4 * p : 4 * p + 4, :]
    for p in range(THIN):
        n = 4 * WIDE + 2 * p
        T[WIDE + p, BASE - 2 : BASE, :] = south[n : n + 2, :]
        T[WIDE + p, top : top + 2, :] = north[n : n + 2, :]
    y_phase(T, E, F, A, WY, tuple((BASE - 8 + i, 48) for i in range(0, total + 16, 48)))

    def tile(i, carry):
        a = pl.multiple_of(i * 16, 16)
        finish(T, A, WY, U, INV, FAC, coef, (o0, o1, o2, o3), a + BASE, a, 16)
        return carry

    lax.fori_loop(0, total // 16, tile, 0)


def vspec():
    return pl.BlockSpec(memory_space=pltpu.VMEM)


def sspec():
    return pl.BlockSpec(memory_space=pltpu.SMEM)


def shards(heat, salt, east, north, water, mx, my, idf, spreading, mirror):
    f32 = jnp.float32
    total = heat.shape[1]
    lon_n, lat_n = lax.axis_size("lon"), lax.axis_size("lat")
    layers = lon_n // LOW
    fields = (heat, salt, east, north)
    tile = mirror[:1] // LANES
    stack = jax.ShapeDtypeStruct((3, total, LANES), f32)
    msg = jax.ShapeDtypeStruct((MSG, LANES), f32)

    def vm(*shape):
        return pltpu.VMEM((*shape, LANES), f32)

    def dma(n):
        return pltpu.SemaphoreType.DMA((n,))

    halos = pl.pallas_call(
        functools.partial(halo_kernel, lon_n, lat_n),
        out_shape=[stack] * 3 + [msg] * 2,
        in_specs=[sspec()] + [vspec()] * 7,
        out_specs=[vspec()] * 5,
        scratch_shapes=[vm(3, total)] * 3
        + [vm(PLANES, 16), vm(7, 16)]
        + [vm(MSG)] * 4
        + [vm(LOW, MSG), vm(layers, MSG), vm(MSG)]
        + [dma(6), dma(6), dma(2), dma(2), dma(LOW), dma(LOW), dma(layers), dma(layers)],
        compiler_params=pltpu.CompilerParams(
            collective_id=0, has_side_effects=True, vmem_limit_bytes=VMEM_LIMIT
        ),
    )(tile, *fields, water, mx, my)

    tall = total + 2 * BASE
    out = jax.ShapeDtypeStruct((8, total, LANES), f32)
    outs = pl.pallas_call(
        step_kernel,
        out_shape=[out] * 4,
        in_specs=[sspec()] + [vspec()] * 13,
        out_specs=[vspec()] * 4,
        scratch_shapes=[vm(PLANES, tall), vm(7, total), vm(4, tall), vm(4, tall), vm(WIDE, tall), vm(8, tall)]
        + [vm(7, total), vm(8, total), vm(7, total)],
        compiler_params=pltpu.CompilerParams(vmem_limit_bytes=VMEM_LIMIT),
    )(spreading, *fields, water, mx, my, *halos, idf)
    return tuple(outs)


def solution(mesh):
    deep = P(None, "lat", "lon")
    flat = P("lat", "lon")
    return jax.shard_map(
        shards,
        mesh=mesh,
        in_specs=(deep,) * 5 + (flat, flat, deep, P(), P("lon")),
        out_specs=(deep,) * 4,
        check_vma=False,
    )
```

```python
import functools

import jax
import jax.numpy as jnp
from jax import lax
from jax.experimental import pallas as pl
from jax.experimental.pallas import tpu as pltpu
from jax.sharding import PartitionSpec as P

LANES = 128
SP, VM, VMP, WET, WETP, MY, MYP, WX, WXP, PLANES = 32, 34, 42, 43, 51, 52, 53, 54, 62, 63
WIDE, THIN = 34, 20
MSG = WIDE * 4 + THIN * 2
VMEM_LIMIT = 56 * 1024 * 1024


def lane_of(rows):
    return lax.broadcasted_iota(jnp.int32, (rows, LANES), 1)


def roll(x, s):
    if isinstance(s, int):
        s = s % LANES
        if s == 0:
            return x
    return pltpu.roll(x, s, 1)


def shifted(q, halo, s, lane):
    if s > 0:
        return roll(jnp.where(lane < s, halo, q), -s)
    return roll(jnp.where(lane >= LANES + s, halo, q), -s)


def group_roll(x, g):
    return pltpu.roll(x, (LANES - 8 * g) % LANES, 1)


def coefs(courant, opening):
    a = jnp.abs(courant)
    ak = a * (1.0 - (2.0 / 3.0) * a)
    cc = courant * opening
    return (
        cc * (1.0 - 0.5 * a - 1.5 * ak),
        cc * (0.5 * a - 1.5 * ak),
        cc * (3.0 * ak),
        courant >= 0.0,
    )


def edge(qm, q0, q1, q2):
    return (7.0 / 12.0) * (q0 + q1) - (1.0 / 12.0) * (qm + q2)


def flux(cf, em, e0, e1, q0, q1):
    a0, a1, a2, up = cf
    return a0 * e0 + a1 * jnp.where(up, em, e1) + a2 * jnp.where(up, q0, q1)


def pack_array(a, refs, wet_ref, mx_ref, my_ref, c_ref):
    rows = 32
    total = c_ref.shape[1]
    lane = lane_of(rows)
    group = ((lane + 4) % LANES) // 8

    def chunk(i, carry):
        r = pl.ds(pl.multiple_of(i * rows, rows), rows)
        wets = [wet_ref[k, r, :].astype(jnp.float32) for k in range(8)]
        acc = jnp.zeros((rows, LANES), jnp.float32)
        if a < 2:
            items = [refs[2 * a + h][k, r, :] * wets[k] for h in range(2) for k in range(8)]
        else:
            items = wets + [mx_ref[r, :], my_ref[r, :]]
        for g, x in enumerate(items):
            acc = jnp.where(group == g, roll(x, 8 * g), acc)
        c_ref[a, r, :] = acc
        return carry

    lax.fori_loop(0, total // rows, chunk, 0)


def packed_x(c_ref, l_ref, r_ref, T, get, tr, rows):
    lane = lane_of(rows)
    low = lane % 8 < 4
    place = (lane + 4) % LANES
    half = place < 64
    group = place // 8
    parts = []
    for right in (True, False):
        near, far = (c_ref, r_ref) if right else (l_ref, c_ref)
        e = [jnp.where(low, get(far, a), get(near, a)) for a in range(3)]

        def both(x, first):
            y = pltpu.roll(x, 64, 1)
            return jnp.where(half, x, y) if first else jnp.where(half, y, x)

        def spread(x, g):
            x = jnp.where(group == g, x, 0.0)
            for s in (8, 16, 32, 64):
                x = x + pltpu.roll(x, s, 1)
            return x

        u, v, wet = both(e[1], True), both(e[1], False), both(e[2], True)
        mx, my = spread(e[2], 8), spread(e[2], 9)
        um = u * mx
        opening = wet * roll(wet, -1)
        weight = 0.5 * (mx + roll(mx, -1)) * opening
        cf = coefs(0.5 * (um + roll(um, -1)), opening)
        starred, fluxes, edges = [], [], []
        for a in range(2):
            q = e[a]
            q1 = roll(q, -1)
            ed = edge(roll(q, 1), q, q1, roll(q, -2))
            f = flux(cf, roll(ed, 1), ed, roll(ed, -1), q, q1)
            starred.append(q + roll(f, 1) - f)
            fluxes.append(f)
            edges.append(ed)
        parts.append((starred, fluxes, edges, weight, v * my, wet, my))
    (rs, _, re, _, rvm, rwet, rmy), (ls, lf, le, lw, lvm, lwet, lmy) = parts
    for a in range(2):
        T[SP + a, tr, :] = jnp.where(low, rs[a], ls[a])
    T[VMP, tr, :] = jnp.where(low, rvm, lvm)
    T[WETP, tr, :] = jnp.where(low, rwet, lwet)
    T[MYP, tr, :] = jnp.where(low, rmy, lmy)
    T[WXP, tr, :] = lw
    return lf, [jnp.where(low, re[a], le[a]) for a in range(2)]


CHUNK = 16


def x_prepare(mx_ref, my_ref, c_ref, l_ref, r_ref, T, H, get, base, count):
    lane = lane_of(CHUNK)
    low = lane % 8 < 4
    for c in range(count):
        tr, hr = pl.ds(base + CHUNK * c, CHUNK), pl.ds(CHUNK * c, CHUNK)
        lf, le = packed_x(c_ref, l_ref, r_ref, T, functools.partial(get, c), tr, CHUNK)
        for a in range(3):
            h = jnp.where(low, get(c, r_ref, a), get(c, l_ref, a))
            H[a, hr, :] = h
        for a in range(2):
            H[3 + a, hr, :] = lf[a]
            H[5 + a, hr, :] = le[a]
        T[MY, tr, :] = get(c, my_ref)
        mxh = group_roll(h, 8)
        H[7, hr, :] = mxh
        H[8, hr, :] = shifted(get(c, mx_ref), mxh, 1, lane)


def x_levels(fields, wet_ref, mx_ref, my_ref, T, H, get, base, count, first, end, unroll):
    lane = lane_of(CHUNK)

    def part(k, c):
        tr, hr = pl.ds(base + CHUNK * c, CHUNK), pl.ds(CHUNK * c, CHUNK)
        mx, mxh, mx1 = get(c, mx_ref), H[7, hr, :], H[8, hr, :]
        wet = get(c, wet_ref, k).astype(jnp.float32)
        T[WET + k, tr, :] = wet
        hwet = group_roll(H[2, hr, :], k)
        opening = wet * shifted(wet, hwet, 1, lane)
        T[WX + k, tr, :] = 0.5 * (mx + mx1) * opening
        hu = group_roll(H[1, hr, :], k)
        um = get(c, fields[2], k) * wet * mx
        cf = coefs(0.5 * (um + shifted(um, hu * mxh, 1, lane)), opening)
        for f in range(4):
            q = get(c, fields[f], k) * wet
            if f == 3:
                T[VM + k, tr, :] = q * get(c, my_ref)
            g = 8 * (f % 2) + k
            h = hu if f == 2 else group_roll(H[f // 2, hr, :], g)
            qm, q1, q2 = (shifted(q, h, s, lane) for s in (-1, 1, 2))
            ed = edge(qm, q, q1, q2)
            he = group_roll(H[5 + f // 2, hr, :], g)
            em = roll(jnp.where(lane == LANES - 1, he, ed), 1)
            e1 = roll(jnp.where(lane == 0, he, ed), -1)
            fl = flux(cf, em, ed, e1, q, q1)
            flm = roll(jnp.where(lane == LANES - 1, group_roll(H[3 + f // 2, hr, :], g), fl), 1)
            T[8 * f + k, tr, :] = q + flm - fl

    def levels(i, carry):
        for j in range(unroll):
            for c in range(count):
                part(i * unroll + j, c)
        return carry

    lax.fori_loop(first // unroll, end // unroll, levels, 0)


def face_y(T, vm, wet, my, WY, kw, r0, rows):
    r, r1 = pl.ds(r0, rows), pl.ds(r0 + 1, rows)
    opening = T[wet, r, :] * T[wet, r1, :]
    if WY is not None:
        WY[kw, r, :] = 0.5 * (T[my, r, :] + T[my, r1, :]) * opening
    return coefs(0.5 * (T[vm, r, :] + T[vm, r1, :]), opening)


def y_advect(T, E, F, A, WY, planes, vm, wet, my, kw, chunks):
    for r0, rows in chunks:
        for n, p in enumerate(planes):
            E[n, pl.ds(r0, rows), :] = edge(*(T[p, pl.ds(r0 + s, rows), :] for s in (-1, 0, 1, 2)))
    for r0, rows in chunks:
        cf = face_y(T, vm, wet, my, WY, kw, r0, rows)
        for n, p in enumerate(planes):
            em, e0, e1 = (E[n, pl.ds(r0 + s, rows), :] for s in (-1, 0, 1))
            q0, q1 = (T[p, pl.ds(r0 + s, rows), :] for s in (0, 1))
            F[n, pl.ds(r0, rows), :] = flux(cf, em, e0, e1, q0, q1)
    for r0, rows in chunks:
        for n, p in enumerate(planes):
            r = pl.ds(r0, rows)
            A[p, r, :] = T[p, r, :] + F[n, pl.ds(r0 - 1, rows), :] - F[n, r, :]


def y_phase(T, E, F, A, WY, chunks):
    y_advect(T, E, F, A, None, (SP, SP + 1), VMP, WETP, MYP, 0, chunks)

    def level(k, carry):
        y_advect(T, E, F, A, WY, tuple(8 * f + k for f in range(4)), VM + k, WET + k, MY, k, chunks)
        return carry

    lax.fori_loop(0, 8, level, 0)


def factorize(T, idf_ref, U, INV, FAC, base, rows):
    r = pl.ds(base, rows)
    wet = T[WET, r, :]
    up, factor = None, None
    for k in range(8):
        divisor = 1.0
        if k > 0:
            divisor = divisor + up * (1.0 - factor)
        if k < 7:
            below = T[WET + k + 1, r, :]
            down = idf_ref[k] * wet * below
            wet = below
            U[k] = down
            divisor = divisor + down
        inv = 1.0 / divisor
        INV[k] = inv
        if k < 7:
            factor = down * inv
            FAC[k] = factor
            up = down


def finish(T, A, WY, U, INV, FAC, coef_ref, outs, t0, o0, rows):
    lane = lane_of(rows)
    r, rp, rm = pl.ds(t0, rows), pl.ds(t0 + 1, rows), pl.ds(t0 - 1, rows)
    o = pl.ds(o0, rows)
    wxp = T[WXP, r, :]
    ap = [A[SP + a, r, :] for a in range(2)]
    reduced = []
    for k in range(8):
        wx = T[WX + k, r, :]
        wxm = roll(jnp.where(lane == LANES - 1, roll(wxp, -8 * k), wx), 1)
        wy, wym = WY[k, r, :], WY[k, rm, :]
        inv = INV[k, o, :]
        row = []
        for f in range(4):
            p = 8 * f + k
            a = A[p, r, :]
            h = roll(ap[f // 2], -8 * (8 * (f % 2) + k))
            a1 = roll(jnp.where(lane == 0, h, a), -1)
            am = roll(jnp.where(lane == LANES - 1, h, a), 1)
            lap = wx * (a1 - a) - wxm * (a - am) + wy * (A[p, rp, :] - a) - wym * (a - A[p, rm, :])
            d = a + coef_ref[f, k] * lap
            if k > 0:
                d = d + U[k - 1, o, :] * reduced[-1][f]
            row.append(d * inv)
        reduced.append(row)
    x = reduced[7]
    for k in range(7, -1, -1):
        if k < 7:
            factor = FAC[k, o, :]
            x = [reduced[k][f] + factor * x[f] for f in range(4)]
        wet = T[WET + k, r, :]
        for f in range(4):
            outs[f][k, o, :] = x[f] * wet


LOW = 4
MESH = pl.DeviceIdType.MESH


BASE = 16


def step_kernel(
    lon_n, lat_n, tile, coef, t, s, u, v, wet, mx, my, idf, o0, o1, o2, o3,
    C, L, R, TE, HE, Mn, Ms, FS, FN, RA, RB, back, T, H, E, F, A, WY, U, INV, FAC,
    s_lon, r_lon, s_lat, r_lat, s_a, r_a, s_b, r_b,
):
    total = t.shape[1]
    me = lax.axis_index("lon")
    lat = lax.axis_index("lat")
    right, left = lax.rem(me + 1, lon_n), lax.rem(me + lon_n - 1, lon_n)
    low, high = lax.rem(me, LOW), me // LOW
    layers = lon_n // LOW
    first, last = lat == 0, lat == lat_n - 1
    ring = [left, right]
    ring += [high * LOW + lax.rem(low + d, LOW) for d in range(1, LOW)]
    ring += [lax.rem(high + d, layers) * LOW + low for d in range(1, layers)]
    barrier = pltpu.get_barrier_semaphore()
    for other in ring:
        pl.semaphore_signal(barrier, inc=1, device_id={"lon": other}, device_id_type=MESH)

    @pl.when(jnp.logical_not(first))
    def _():
        pl.semaphore_signal(barrier, inc=1, device_id={"lat": lat - 1}, device_id_type=MESH)

    @pl.when(jnp.logical_not(last))
    def _():
        pl.semaphore_signal(barrier, inc=1, device_id={"lat": lat + 1}, device_id_type=MESH)

    def send(src, dst, ss, rs, where):
        return pltpu.make_async_remote_copy(
            src_ref=src, dst_ref=dst, send_sem=ss, recv_sem=rs, device_id=where, device_id_type=MESH
        )

    fields = (t, s, u, v)
    lon_copies = []
    for a in range(3):
        pack_array(a, fields, wet, mx, my, C)
        if a == 0:
            peers = len(ring) + jnp.where(first, 0, 1) + jnp.where(last, 0, 1)
            pl.semaphore_wait(barrier, peers)
        for dst, where, i in ((R, left, 0), (L, right, 1)):
            cp = send(C.at[a], dst.at[a], s_lon.at[2 * a + i], r_lon.at[2 * a + i], {"lon": where})
            cp.start()
            lon_copies.append(cp)
    for cp in lon_copies:
        cp.wait()

    def ends(c, ref, *k):
        return jnp.concatenate([ref[(*k, pl.ds(0, 8))], ref[(*k, pl.ds(total - 8, 8))]], axis=0)

    def get(c, ref, *k):
        return ref[(*k, pl.ds(CHUNK * c, CHUNK))]

    x_prepare(mx, my, C, L, R, TE, HE, ends, 0, 1)
    x_levels(fields, wet, mx, my, TE, HE, ends, 0, 1, 0, 8, 4)
    for p in range(WIDE):
        Mn[4 * p : 4 * p + 4, :] = TE[p, 12:16, :]
    for p in range(THIN):
        n = 4 * WIDE + 2 * p
        Mn[n : n + 2, :] = TE[WIDE + p, 14:16, :]
    a_copies = []
    for d in range(1, LOW):
        cp = send(Mn, RA.at[low], s_a.at[d], r_a.at[d], {"lon": high * LOW + lax.rem(low + d, LOW)})
        cp.start()
        a_copies.append(cp)
    to_north = send(Mn, FS, s_lat.at[0], r_lat.at[0], {"lat": lat + 1})
    to_south = send(Ms, FN, s_lat.at[1], r_lat.at[1], {"lat": lat - 1})

    @pl.when(jnp.logical_not(last))
    def _():
        to_north.start()

    for p in range(WIDE):
        Ms[4 * p : 4 * p + 4, :] = TE[p, 0:4, :]
    for p in range(THIN):
        n = 4 * WIDE + 2 * p
        Ms[n : n + 2, :] = TE[WIDE + p, 0:2, :]

    @pl.when(jnp.logical_not(first))
    def _():
        to_south.start()

    RA[low] = Mn[...]
    count = total // CHUNK
    x_prepare(mx, my, C, L, R, T, H, get, BASE, count)
    x_levels(fields, wet, mx, my, T, H, get, BASE, count, 0, 2, 1)
    for cp in a_copies:
        cp.wait()
    RB[high] = RA[lax.rem(tile[0], LOW)]
    b_copies = []
    for d in range(1, layers):
        cp = send(RB.at[high], RB.at[high], s_b.at[d], r_b.at[d], {"lon": lax.rem(high + d, layers) * LOW + low})
        cp.start()
        b_copies.append(cp)

    x_levels(fields, wet, mx, my, T, H, get, BASE, count, 2, 8, 1)
    factorize(T, idf, U, INV, FAC, BASE, total)

    def spread(src, wide, thin):
        for p in range(WIDE):
            T[p, wide : wide + 4, :] = src[4 * p : 4 * p + 4, :]
        for p in range(THIN):
            n = 4 * WIDE + 2 * p
            T[WIDE + p, thin : thin + 2, :] = src[n : n + 2, :]

    top = BASE + total

    @pl.when(jnp.logical_not(last))
    def _():
        to_north.wait_send()
        to_south.wait_recv()
        spread(FN, top, top)

    @pl.when(jnp.logical_not(first))
    def _():
        to_south.wait_send()
        to_north.wait_recv()
        spread(FS, BASE - 4, BASE - 2)

    @pl.when(first)
    def _():
        T[:, BASE - 8 : BASE, :] = jnp.zeros((PLANES, 8, LANES), jnp.float32)

    for cp in b_copies:
        cp.wait()

    @pl.when(last)
    def _():
        x = RB[tile[0] // LOW]
        lane = lane_of(MSG)
        row = lax.broadcasted_iota(jnp.int32, (MSG, LANES), 0)
        flip = jnp.take_along_axis(x, LANES - 1 - lane, axis=1)
        swap = jnp.where(lane % 8 == 0, roll(x, 1), roll(x, -1))
        w = 4 * WIDE
        packed = (
            ((row >= 4 * SP) & (row < w))
            | ((row >= w + 2 * (VMP - WIDE)) & (row < w + 2 * (WET - WIDE)))
            | ((row >= w + 2 * (WETP - WIDE)) & (row < w + 2 * (MY - WIDE)))
            | (row >= w + 2 * (MYP - WIDE))
        )
        minus = (
            ((row >= 64) & (row < 4 * SP))
            | ((row >= 4 * SP + 4) & (row < w))
            | ((row >= w) & (row < w + 2 * (WET - WIDE)))
        )
        y = jnp.where(packed, swap, flip)
        back[...] = jnp.where(minus, -y, y)
        for p in range(WIDE):
            for i in range(4):
                T[p, top + i : top + i + 1, :] = back[4 * p + 3 - i : 4 * p + 4 - i, :]
        for p in range(THIN):
            n = w + 2 * p
            for i in range(2):
                T[WIDE + p, top + i : top + i + 1, :] = back[n + 1 - i : n + 2 - i, :]

    y_phase(T, E, F, A, WY, tuple((BASE - 8 + i, 24) for i in range(0, total + 16, 24)))

    def tile_rows(i, carry):
        a = pl.multiple_of(i * 16, 16)
        finish(T, A, WY, U, INV, FAC, coef, (o0, o1, o2, o3), a + BASE, a, 16)
        return carry

    lax.fori_loop(0, total // 16, tile_rows, 0)


def vspec():
    return pl.BlockSpec(memory_space=pltpu.VMEM)


def sspec():
    return pl.BlockSpec(memory_space=pltpu.SMEM)


def shards(heat, salt, east, north, water, mx, my, idf, spreading, mirror):
    total = heat.shape[1]
    lon_n, lat_n = lax.axis_size("lon"), lax.axis_size("lat")
    layers = lon_n // LOW
    fields = (heat, salt, east, north)
    tile = mirror[:1] // LANES
    tall = total + 2 * BASE
    out = jax.ShapeDtypeStruct((8, total, LANES), jnp.float32)

    def vm(*shape):
        return pltpu.VMEM((*shape, LANES), jnp.float32)

    def dma(n):
        return pltpu.SemaphoreType.DMA((n,))

    outs = pl.pallas_call(
        functools.partial(step_kernel, lon_n, lat_n),
        out_shape=[out] * 4,
        in_specs=[sspec(), sspec()] + [vspec()] * 8,
        out_specs=[vspec()] * 4,
        scratch_shapes=[vm(3, total)] * 3
        + [vm(PLANES, 16), vm(9, 16)]
        + [vm(MSG)] * 4
        + [vm(LOW, MSG), vm(layers, MSG), vm(MSG)]
        + [vm(PLANES, tall), vm(9, total), vm(4, tall), vm(4, tall), vm(WIDE, tall), vm(8, tall)]
        + [vm(7, total), vm(8, total), vm(7, total)]
        + [dma(6), dma(6), dma(2), dma(2), dma(LOW), dma(LOW), dma(layers), dma(layers)],
        compiler_params=pltpu.CompilerParams(
            collective_id=0, has_side_effects=True, vmem_limit_bytes=VMEM_LIMIT
        ),
    )(tile, spreading, *fields, water, mx, my, idf)
    return tuple(outs)


def solution(mesh):
    deep = P(None, "lat", "lon")
    flat = P("lat", "lon")
    return jax.shard_map(
        shards,
        mesh=mesh,
        in_specs=(deep,) * 5 + (flat, flat, deep, P(), P("lon")),
        out_specs=(deep,) * 4,
        check_vma=False,
    )
```

```python
import functools

import jax
import jax.numpy as jnp
from jax import lax
from jax.experimental import pallas as pl
from jax.experimental.pallas import tpu as pltpu
from jax.sharding import PartitionSpec as P

LANES = 128
SP, VM, VMP, WET, WETP, MY, MYP, WX, WXP, PLANES = 32, 34, 42, 43, 51, 52, 53, 54, 62, 63
WIDE, THIN = 34, 20
MSG = WIDE * 4 + THIN * 2
VMEM_LIMIT = 32 * 1024 * 1024


def lane_of(rows):
    return lax.broadcasted_iota(jnp.int32, (rows, LANES), 1)


def roll(x, s):
    if isinstance(s, int):
        s = s % LANES
        if s == 0:
            return x
    return pltpu.roll(x, s, 1)


def shifted(q, halo, s, lane):
    if s > 0:
        return roll(jnp.where(lane < s, halo, q), -s)
    return roll(jnp.where(lane >= LANES + s, halo, q), -s)


def group_roll(x, g):
    return pltpu.roll(x, (LANES - 8 * g) % LANES, 1)


def coefs(courant, opening):
    a = jnp.abs(courant)
    ak = a * (1.0 - (2.0 / 3.0) * a)
    cc = courant * opening
    return (
        cc * (1.0 - 0.5 * a - 1.5 * ak),
        cc * (0.5 * a - 1.5 * ak),
        cc * (3.0 * ak),
        courant >= 0.0,
    )


def edge(qm, q0, q1, q2):
    return (7.0 / 12.0) * (q0 + q1) - (1.0 / 12.0) * (qm + q2)


def flux(cf, em, e0, e1, q0, q1):
    a0, a1, a2, up = cf
    return a0 * e0 + a1 * jnp.where(up, em, e1) + a2 * jnp.where(up, q0, q1)


def pack_array(a, refs, wet_ref, mx_ref, my_ref, c_ref):
    rows = 32
    total = c_ref.shape[1]
    lane = lane_of(rows)
    group = ((lane + 4) % LANES) // 8

    def chunk(i, carry):
        r = pl.ds(pl.multiple_of(i * rows, rows), rows)
        wets = [wet_ref[k, r, :].astype(jnp.float32) for k in range(8)]
        acc = jnp.zeros((rows, LANES), jnp.float32)
        if a < 2:
            items = [refs[2 * a + h][k, r, :] * wets[k] for h in range(2) for k in range(8)]
        else:
            items = wets + [mx_ref[r, :], my_ref[r, :]]
        for g, x in enumerate(items):
            acc = jnp.where(group == g, roll(x, 8 * g), acc)
        c_ref[a, r, :] = acc
        return carry

    lax.fori_loop(0, total // rows, chunk, 0)


def packed_x(c_ref, l_ref, r_ref, T, get, tr, rows):
    lane = lane_of(rows)
    low = lane % 8 < 4
    place = (lane + 4) % LANES
    half = place < 64
    group = place // 8
    parts = []
    for right in (True, False):
        near, far = (c_ref, r_ref) if right else (l_ref, c_ref)
        e = [jnp.where(low, get(far, a), get(near, a)) for a in range(3)]

        def both(x, first):
            y = pltpu.roll(x, 64, 1)
            return jnp.where(half, x, y) if first else jnp.where(half, y, x)

        def spread(x, g):
            x = jnp.where(group == g, x, 0.0)
            for s in (8, 16, 32, 64):
                x = x + pltpu.roll(x, s, 1)
            return x

        u, v, wet = both(e[1], True), both(e[1], False), both(e[2], True)
        mx, my = spread(e[2], 8), spread(e[2], 9)
        um = u * mx
        opening = wet * roll(wet, -1)
        weight = 0.5 * (mx + roll(mx, -1)) * opening
        cf = coefs(0.5 * (um + roll(um, -1)), opening)
        starred, fluxes, edges = [], [], []
        for a in range(2):
            q = e[a]
            q1 = roll(q, -1)
            ed = edge(roll(q, 1), q, q1, roll(q, -2))
            f = flux(cf, roll(ed, 1), ed, roll(ed, -1), q, q1)
            starred.append(q + roll(f, 1) - f)
            fluxes.append(f)
            edges.append(ed)
        parts.append((starred, fluxes, edges, weight, v * my, wet, my))
    (rs, _, re, _, rvm, rwet, rmy), (ls, lf, le, lw, lvm, lwet, lmy) = parts
    for a in range(2):
        T[SP + a, tr, :] = jnp.where(low, rs[a], ls[a])
    T[VMP, tr, :] = jnp.where(low, rvm, lvm)
    T[WETP, tr, :] = jnp.where(low, rwet, lwet)
    T[MYP, tr, :] = jnp.where(low, rmy, lmy)
    T[WXP, tr, :] = lw
    return lf, [jnp.where(low, re[a], le[a]) for a in range(2)]


def x_prepare(mx_ref, my_ref, c_ref, l_ref, r_ref, T, H, get, base, count, CHUNK):
    lane = lane_of(CHUNK)
    low = lane % 8 < 4
    for c in range(count):
        tr, hr = pl.ds(base + CHUNK * c, CHUNK), pl.ds(CHUNK * c, CHUNK)
        lf, le = packed_x(c_ref, l_ref, r_ref, T, functools.partial(get, c), tr, CHUNK)
        for a in range(3):
            h = jnp.where(low, get(c, r_ref, a), get(c, l_ref, a))
            H[a, hr, :] = h
        for a in range(2):
            H[3 + a, hr, :] = lf[a]
            H[5 + a, hr, :] = le[a]
        T[MY, tr, :] = get(c, my_ref)
        mxh = group_roll(h, 8)
        H[7, hr, :] = mxh
        H[8, hr, :] = shifted(get(c, mx_ref), mxh, 1, lane)


def x_levels(fields, wet_ref, mx_ref, my_ref, T, H, get, base, count, first, end, unroll, CHUNK):
    lane = lane_of(CHUNK)

    def part(k, c):
        out = []
        tr, hr = pl.ds(base + CHUNK * c, CHUNK), pl.ds(CHUNK * c, CHUNK)
        mx, mxh, mx1 = get(c, mx_ref), H[7, hr, :], H[8, hr, :]
        wet = get(c, wet_ref, k).astype(jnp.float32)
        out.append((WET + k, tr, wet))
        hwet = group_roll(H[2, hr, :], k)
        opening = wet * shifted(wet, hwet, 1, lane)
        out.append((WX + k, tr, 0.5 * (mx + mx1) * opening))
        hu = group_roll(H[1, hr, :], k)
        um = get(c, fields[2], k) * wet * mx
        cf = coefs(0.5 * (um + shifted(um, hu * mxh, 1, lane)), opening)
        for f in range(4):
            q = get(c, fields[f], k) * wet
            if f == 3:
                out.append((VM + k, tr, q * get(c, my_ref)))
            g = 8 * (f % 2) + k
            h = hu if f == 2 else group_roll(H[f // 2, hr, :], g)
            qm, q1, q2 = (shifted(q, h, s, lane) for s in (-1, 1, 2))
            ed = edge(qm, q, q1, q2)
            he = group_roll(H[5 + f // 2, hr, :], g)
            em = roll(jnp.where(lane == LANES - 1, he, ed), 1)
            e1 = roll(jnp.where(lane == 0, he, ed), -1)
            fl = flux(cf, em, ed, e1, q, q1)
            flm = roll(jnp.where(lane == LANES - 1, group_roll(H[3 + f // 2, hr, :], g), fl), 1)
            out.append((8 * f + k, tr, q + flm - fl))

        return out

    def levels(i, carry):
        for c in range(count):
            stores = []
            for j in range(unroll):
                stores += part(i * unroll + j, c)
            for p, tr, x in stores:
                T[p, tr, :] = x
        return carry

    lax.fori_loop(first // unroll, end // unroll, levels, 0)


def y_advect(T, A, WY, planes, vm, wet, my, kw, r0, rows):
    f0, fr = r0 - 8, rows + 8
    at = pl.ds(f0, fr)
    a1 = pl.ds(f0 + 1, fr)
    opening = T[wet, at, :] * T[wet, a1, :]
    cf = coefs(0.5 * (T[vm, at, :] + T[vm, a1, :]), opening)
    stores = []
    if WY is not None:
        stores.append((WY, kw, at, 0.5 * (T[my, at, :] + T[my, a1, :]) * opening))
    for p in planes:
        q = [T[p, pl.ds(f0 + s, fr), :] for s in (-2, -1, 0, 1, 2, 3)]
        em, e0, e1 = (edge(*q[i : i + 4]) for i in range(3))
        fl = flux(cf, em, e0, e1, q[2], q[3])
        stores.append((A, p, pl.ds(r0, rows), q[2][8:] + fl[7 : 7 + rows] - fl[8:]))
    for ref, p, r, x in stores:
        ref[p, r, :] = x


def y_phase(T, A, WY, chunks):
    for r0, rows in chunks:
        y_advect(T, A, None, (SP, SP + 1), VMP, WETP, MYP, 0, r0, rows)

    def level(k, carry):
        for r0, rows in chunks:
            y_advect(T, A, WY, tuple(8 * f + k for f in range(4)), VM + k, WET + k, MY, k, r0, rows)
        return carry

    lax.fori_loop(0, 8, level, 0)


def factorize(T, idf_ref, U, INV, FAC, base, rows):
    r = pl.ds(base, rows)
    wet = T[WET, r, :]
    up, factor = None, None
    for k in range(8):
        divisor = 1.0
        if k > 0:
            divisor = divisor + up * (1.0 - factor)
        if k < 7:
            below = T[WET + k + 1, r, :]
            down = idf_ref[k] * wet * below
            wet = below
            U[k] = down
            divisor = divisor + down
        inv = 1.0 / divisor
        INV[k] = inv
        if k < 7:
            factor = down * inv
            FAC[k] = factor
            up = down


def finish(T, A, WY, U, INV, FAC, coef_ref, outs, t0, o0, rows):
    lane = lane_of(rows)
    r, rp, rm = pl.ds(t0, rows), pl.ds(t0 + 1, rows), pl.ds(t0 - 1, rows)
    o = pl.ds(o0, rows)
    wxp = T[WXP, r, :]
    ap = [A[SP + a, r, :] for a in range(2)]
    reduced = []
    wets = [T[WET + k, r, :] for k in range(8)]
    facs = [FAC[k, o, :] for k in range(7)]
    for k in range(8):
        wx = T[WX + k, r, :]
        wxm = roll(jnp.where(lane == LANES - 1, roll(wxp, -8 * k), wx), 1)
        wy, wym = WY[k, r, :], WY[k, rm, :]
        inv = INV[k, o, :]
        row = []
        for f in range(4):
            p = 8 * f + k
            a = A[p, r, :]
            h = roll(ap[f // 2], -8 * (8 * (f % 2) + k))
            a1 = roll(jnp.where(lane == 0, h, a), -1)
            am = roll(jnp.where(lane == LANES - 1, h, a), 1)
            lap = wx * (a1 - a) - wxm * (a - am) + wy * (A[p, rp, :] - a) - wym * (a - A[p, rm, :])
            d = a + coef_ref[f, k] * lap
            if k > 0:
                d = d + U[k - 1, o, :] * reduced[-1][f]
            row.append(d * inv)
        reduced.append(row)
    solved = [reduced[7]]
    for k in range(6, -1, -1):
        solved.insert(0, [reduced[k][f] + facs[k] * solved[0][f] for f in range(4)])
    for k in range(8):
        for f in range(4):
            outs[f][k, o, :] = solved[k][f] * wets[k]


LOW = 4
MESH = pl.DeviceIdType.MESH


BASE = 24


def zonal_kernel(
    lon_n, lat_n, tile, t, s, u, v, wet, mx, my, T,
    C, L, R, TE, HE, Mn, Ms, FS, FN, RA, RB, back, H,
    s_lon, r_lon, s_lat, r_lat, s_a, r_a, s_b, r_b,
):
    total = t.shape[1]
    me = lax.axis_index("lon")
    lat = lax.axis_index("lat")
    right, left = lax.rem(me + 1, lon_n), lax.rem(me + lon_n - 1, lon_n)
    low, high = lax.rem(me, LOW), me // LOW
    layers = lon_n // LOW
    first, last = lat == 0, lat == lat_n - 1
    ring = [left, right]
    ring += [high * LOW + lax.rem(low + d, LOW) for d in range(1, LOW)]
    ring += [lax.rem(high + d, layers) * LOW + low for d in range(1, layers)]
    barrier = pltpu.get_barrier_semaphore()
    for other in ring:
        pl.semaphore_signal(barrier, inc=1, device_id={"lon": other}, device_id_type=MESH)

    @pl.when(jnp.logical_not(first))
    def _():
        pl.semaphore_signal(barrier, inc=1, device_id={"lat": lat - 1}, device_id_type=MESH)

    @pl.when(jnp.logical_not(last))
    def _():
        pl.semaphore_signal(barrier, inc=1, device_id={"lat": lat + 1}, device_id_type=MESH)

    def send(src, dst, ss, rs, where):
        return pltpu.make_async_remote_copy(
            src_ref=src, dst_ref=dst, send_sem=ss, recv_sem=rs, device_id=where, device_id_type=MESH
        )

    fields = (t, s, u, v)
    lon_copies = []
    for a in range(3):
        pack_array(a, fields, wet, mx, my, C)
        if a == 0:
            peers = len(ring) + jnp.where(first, 0, 1) + jnp.where(last, 0, 1)
            pl.semaphore_wait(barrier, peers)
        for dst, where, i in ((R, left, 0), (L, right, 1)):
            cp = send(C.at[a], dst.at[a], s_lon.at[2 * a + i], r_lon.at[2 * a + i], {"lon": where})
            cp.start()
            lon_copies.append(cp)
    for cp in lon_copies:
        cp.wait()

    def ends(c, ref, *k):
        return jnp.concatenate([ref[(*k, pl.ds(0, 8))], ref[(*k, pl.ds(total - 8, 8))]], axis=0)

    def get(c, ref, *k):
        return ref[(*k, pl.ds(64 * c, 64))]

    x_prepare(mx, my, C, L, R, TE, HE, ends, 0, 1, 16)
    x_levels(fields, wet, mx, my, TE, HE, ends, 0, 1, 0, 8, 4, 16)
    for p in range(WIDE):
        Mn[4 * p : 4 * p + 4, :] = TE[p, 12:16, :]
    for p in range(THIN):
        n = 4 * WIDE + 2 * p
        Mn[n : n + 2, :] = TE[WIDE + p, 14:16, :]
    a_copies = []
    for d in range(1, LOW):
        cp = send(Mn, RA.at[low], s_a.at[d], r_a.at[d], {"lon": high * LOW + lax.rem(low + d, LOW)})
        cp.start()
        a_copies.append(cp)
    to_north = send(Mn, FS, s_lat.at[0], r_lat.at[0], {"lat": lat + 1})
    to_south = send(Ms, FN, s_lat.at[1], r_lat.at[1], {"lat": lat - 1})

    @pl.when(jnp.logical_not(last))
    def _():
        to_north.start()

    for p in range(WIDE):
        Ms[4 * p : 4 * p + 4, :] = TE[p, 0:4, :]
    for p in range(THIN):
        n = 4 * WIDE + 2 * p
        Ms[n : n + 2, :] = TE[WIDE + p, 0:2, :]

    @pl.when(jnp.logical_not(first))
    def _():
        to_south.start()

    RA[low] = Mn[...]
    count = total // 64
    x_prepare(mx, my, C, L, R, T, H, get, BASE, count, 64)
    x_levels(fields, wet, mx, my, T, H, get, BASE, count, 0, 2, 1, 64)
    for cp in a_copies:
        cp.wait()
    RB[high] = RA[lax.rem(tile[0], LOW)]
    b_copies = []
    for d in range(1, layers):
        cp = send(RB.at[high], RB.at[high], s_b.at[d], r_b.at[d], {"lon": lax.rem(high + d, layers) * LOW + low})
        cp.start()
        b_copies.append(cp)

    x_levels(fields, wet, mx, my, T, H, get, BASE, count, 2, 8, 1, 64)

    def spread(src, wide, thin):
        for p in range(WIDE):
            T[p, wide : wide + 4, :] = src[4 * p : 4 * p + 4, :]
        for p in range(THIN):
            n = 4 * WIDE + 2 * p
            T[WIDE + p, thin : thin + 2, :] = src[n : n + 2, :]

    top = BASE + total

    @pl.when(jnp.logical_not(last))
    def _():
        to_north.wait_send()
        to_south.wait_recv()
        spread(FN, top, top)

    @pl.when(jnp.logical_not(first))
    def _():
        to_south.wait_send()
        to_north.wait_recv()
        spread(FS, BASE - 4, BASE - 2)

    @pl.when(first)
    def _():
        T[:, BASE - 8 : BASE, :] = jnp.zeros((PLANES, 8, LANES), jnp.float32)

    for cp in b_copies:
        cp.wait()

    @pl.when(last)
    def _():
        x = RB[tile[0] // LOW]
        lane = lane_of(MSG)
        row = lax.broadcasted_iota(jnp.int32, (MSG, LANES), 0)
        flip = jnp.take_along_axis(x, LANES - 1 - lane, axis=1)
        swap = jnp.where(lane % 8 == 0, roll(x, 1), roll(x, -1))
        w = 4 * WIDE
        packed = (
            ((row >= 4 * SP) & (row < w))
            | ((row >= w + 2 * (VMP - WIDE)) & (row < w + 2 * (WET - WIDE)))
            | ((row >= w + 2 * (WETP - WIDE)) & (row < w + 2 * (MY - WIDE)))
            | (row >= w + 2 * (MYP - WIDE))
        )
        minus = (
            ((row >= 64) & (row < 4 * SP))
            | ((row >= 4 * SP + 4) & (row < w))
            | ((row >= w) & (row < w + 2 * (WET - WIDE)))
        )
        y = jnp.where(packed, swap, flip)
        back[...] = jnp.where(minus, -y, y)
        for p in range(WIDE):
            for i in range(4):
                T[p, top + i : top + i + 1, :] = back[4 * p + 3 - i : 4 * p + 4 - i, :]
        for p in range(THIN):
            n = w + 2 * p
            for i in range(2):
                T[WIDE + p, top + i : top + i + 1, :] = back[n + 1 - i : n + 2 - i, :]


def meridional_kernel(coef, T, idf, o0, o1, o2, o3, A, WY, U, INV, FAC):
    total = idf.shape[1]
    factorize(T, idf, U, INV, FAC, BASE, total)
    y_phase(T, A, WY, tuple((BASE - 8 + i, 48) for i in range(0, total + 16, 48)))

    def tile_rows(i, carry):
        a = pl.multiple_of(i * 16, 16)
        finish(T, A, WY, U, INV, FAC, coef, (o0, o1, o2, o3), a + BASE, a, 16)
        return carry

    lax.fori_loop(0, total // 16, tile_rows, 0)


def vspec():
    return pl.BlockSpec(memory_space=pltpu.VMEM)


def sspec():
    return pl.BlockSpec(memory_space=pltpu.SMEM)


def shards(heat, salt, east, north, water, mx, my, idf, spreading, mirror):
    total = heat.shape[1]
    lon_n, lat_n = lax.axis_size("lon"), lax.axis_size("lat")
    layers = lon_n // LOW
    fields = (heat, salt, east, north)
    tile = mirror[:1] // LANES
    tall = total + 2 * BASE
    out = jax.ShapeDtypeStruct((8, total, LANES), jnp.float32)

    def vm(*shape):
        return pltpu.VMEM((*shape, LANES), jnp.float32)

    def dma(n):
        return pltpu.SemaphoreType.DMA((n,))

    stack = pl.pallas_call(
        functools.partial(zonal_kernel, lon_n, lat_n),
        out_shape=jax.ShapeDtypeStruct((PLANES, tall, LANES), jnp.float32),
        in_specs=[sspec()] + [vspec()] * 7,
        out_specs=vspec(),
        scratch_shapes=[vm(3, total)] * 3
        + [vm(PLANES, 16), vm(9, 16)]
        + [vm(MSG)] * 4
        + [vm(LOW, MSG), vm(layers, MSG), vm(MSG)]
        + [vm(9, total)]
        + [dma(6), dma(6), dma(2), dma(2), dma(LOW), dma(LOW), dma(layers), dma(layers)],
        compiler_params=pltpu.CompilerParams(
            collective_id=0, has_side_effects=True, vmem_limit_bytes=VMEM_LIMIT
        ),
    )(tile, *fields, water, mx, my)
    outs = pl.pallas_call(
        meridional_kernel,
        out_shape=[out] * 4,
        in_specs=[sspec()] + [vspec()] * 2,
        out_specs=[vspec()] * 4,
        scratch_shapes=[vm(WIDE, tall), vm(8, tall), vm(7, total), vm(8, total), vm(7, total)],
        compiler_params=pltpu.CompilerParams(vmem_limit_bytes=VMEM_LIMIT),
    )(spreading, stack, idf)
    return tuple(outs)


def solution(mesh):
    deep = P(None, "lat", "lon")
    flat = P("lat", "lon")
    return jax.shard_map(
        shards,
        mesh=mesh,
        in_specs=(deep,) * 5 + (flat, flat, deep, P(), P("lon")),
        out_specs=(deep,) * 4,
        check_vma=False,
    )
```
